32 devices in a mesh: row: 4 (over y, core), col: 8 (over z, x).
Axes of the slice: x: 2, y: 2, z: 4, core: 2. Of those that a mesh axis runs over, the one named last changes fastest.
Arguments:
- features: bfloat16 [16384, 256], P(('row', 'col')), may hold values from -6 to 6
- w_self: bfloat16 [256, 256], replicated, may hold values from -0.375 to 0.375
- w_neigh: bfloat16 [256, 256], replicated, may hold values from -3 to 3
- cotangent: bfloat16 [16384, 256], P(('row', 'col')), may hold values from -6 to 6
- degree: int32 [16384], P(('row', 'col')), may hold values from 64 to 256
- tile_rows: int32 [8192], P(('row', 'col')), may hold values from 0 to 31
- tile_cols: int32 [8192], P(('row', 'col')), may hold values from 0 to 15
- tile_edges: int32 [4, 8192, 128], P(None, ('row', 'col')), may hold values from 0 to 127
- tile_count: int32 [32], P(('row', 'col')), may hold values from 4 to 256, as said below
Outputs:
- activations: bfloat16 [16384, 256], P(('row', 'col'))
- feature_grad: bfloat16 [16384, 256], P(('row', 'col'))
- grad_self: float32 [256, 256], replicated
- grad_neigh: float32 [256, 256], replicated
The draws below stay inside these ranges and needn't reach their ends.
Inputs may be any that keep to these rules, and one draw needn't show every extreme that they name: The busiest device uses all 256 of its slots; slots from tile_count on are ignored.
All inputs are finite; a program needn't handle non-finite values.
Results may differ from the reference program's by a relative error of at most 0.0059.
Values may be sent and summed in bfloat16 or wider, within the bound.
A program may use at most 64 MiB of HBM per device.

```python
import math
import jax
import jax.numpy as jnp
import numpy as np
from jax import lax

F = 256
TILE = 128
EDGE_K = 4
TPD = 4
CAP = 256
ROWT = 32
COLT = 16
NODES = 16384
TILES = 8192
N_ROW = 4
N_COL = 8


def draw_tile_count(key, part):
    weights = jax.random.randint(key, (N_ROW * N_COL,), 1, 9)
    weights = weights * weights
    largest = jnp.max(weights)
    return (weights * CAP // largest).astype(jnp.int32)


def set_ends(entries, stream_key, smallest, high):
    shape = entries.shape
    place = [jax.random.randint(jax.random.fold_in(stream_key, axis), (), 0, shape[axis]) for axis in range(len(shape))]
    entries = entries.at[tuple(place)].set(smallest)
    longest = shape.index(max(shape))
    place[longest] = (place[longest] + 1) % shape[longest]
    return entries.at[tuple(place)].set(high)


def block_scale(stream_key, dims, split, smallest, high):
    def one(position, blocks):
        heights = jax.random.uniform(jax.random.fold_in(jax.random.fold_in(stream_key, 6), position), (blocks,), jnp.float32, smallest / len(split), high / len(split))
        return jnp.repeat(jnp.exp(heights), dims[position] // blocks).reshape((-1,) + (1,) * (len(dims) - position - 1))

    gain = one(*split[0])
    for cut in split[1:]:
        gain = gain * one(*cut)
    return gain


def rank_bounds(amount, skew):
    weights = [(1 << 20) // math.isqrt(grade ** skew) + 1 for grade in range(1, amount + 1)]
    scale = 1 + sum(weights) // (1 << 30)
    return np.cumsum(np.array([max(1, weight // scale) for weight in weights]))


def ranked(rng, dims, count, skew):
    table = rank_bounds(count, skew)
    pick = jax.random.randint(jax.random.fold_in(rng, 1), dims, 0, int(table[count - 1]))
    grade = jnp.searchsorted(jnp.asarray(table, jnp.int32), pick, side="right")
    return jax.random.permutation(jax.random.fold_in(rng, 2), count)[grade].astype(jnp.int32)


def normal_values(rng, extent, deviation, reach, shards=(), kind=jnp.bfloat16):
    entries = jax.random.normal(rng, extent, jnp.float32) * deviation
    if len(shards) > 0:
        entries = block_scale(rng, extent, shards, -0.22, 0.18) * entries
    return jnp.clip(entries, min=-reach, max=reach).astype(kind)


def setup_inputs(seed: int = 0) -> dict:
    splits = jax.random.split(jax.random.key(seed), 10)
    return {
        "features": normal_values(splits[0], (NODES, F), 1.0, 6.0, ((0, 32),)),
        "w_self": normal_values(splits[1], (F, F), F ** -0.5, 0.375),
        "w_neigh": normal_values(splits[2], (F, F), (max(F // 64, 1)) ** -0.5, 3.0),
        "cotangent": normal_values(splits[3], (NODES, F), 1.0, 6.0, ((0, 32),)),
        "degree": set_ends(jax.random.randint(splits[4], (NODES,), CAP * EDGE_K // (4 * TPD), CAP * EDGE_K // TPD + 1), jax.random.fold_in(splits[4], 1), CAP * EDGE_K // (4 * TPD), (CAP * EDGE_K // TPD + 1) - 1).astype(jnp.int32),
        "tile_rows": set_ends(ranked(splits[5], (TILES,), ROWT, 2), jax.random.fold_in(splits[5], 3), 0, ROWT - 1).astype(jnp.int32),
        "tile_cols": set_ends(jax.random.randint(splits[6], (TILES,), 0, COLT), jax.random.fold_in(splits[6], 1), 0, COLT - 1).astype(jnp.int32),
        "tile_edges": set_ends(jax.random.randint(splits[7], (EDGE_K, TILES, TILE), 0, TILE), jax.random.fold_in(splits[7], 1), 0, TILE - 1).astype(jnp.int32),
        "tile_count": draw_tile_count(jax.random.fold_in(splits[9], 71), 0),
    }


def device_edges(device, tile_rows, tile_cols, tile_edges, tile_count):
    row_index = device // N_COL
    col_index = device % N_COL
    first_slot = (device * CAP).astype(jnp.int32)
    slot_rows = lax.dynamic_slice_in_dim(tile_rows, first_slot, CAP)
    slot_cols = lax.dynamic_slice_in_dim(tile_cols, first_slot, CAP)
    slot_edges = lax.dynamic_slice_in_dim(tile_edges, first_slot, CAP, axis=1)
    in_use = (jnp.arange(CAP, dtype=jnp.int32) < tile_count[device]).astype(jnp.float32)
    global_rows = row_index * (N_COL * TPD) + slot_rows
    global_cols = (slot_cols // TPD * N_COL + col_index) * TPD + slot_cols % TPD
    offsets = jnp.arange(TILE, dtype=jnp.int32)
    targets = global_rows[:, None] * TILE + offsets[None, :]
    sources = global_cols[None, :, None] * TILE + slot_edges
    return (targets, sources, in_use)

def reference(features, w_self, w_neigh, cotangent, degree, tile_rows, tile_cols, tile_edges, tile_count):
    devices_all = jnp.arange(N_ROW * N_COL, dtype=jnp.int32)
    feats_wide = features.astype(jnp.float32)

    def gather_step(running, device):
        targets, sources, in_use = device_edges(device, tile_rows, tile_cols, tile_edges, tile_count)
        message = lax.optimization_barrier(jnp.sum(feats_wide[sources], axis=0)) * in_use[:, None, None]
        return (running.at[targets.reshape(-1)].add(message.reshape(-1, F)), None)
    neighbour_sum, _ = lax.scan(gather_step, jnp.zeros((NODES, F), jnp.float32), devices_all)
    degree_wide = degree.astype(jnp.float32)[:, None]
    aggregate = (neighbour_sum / degree_wide).astype(jnp.bfloat16)
    preact = jnp.dot(features, w_self, preferred_element_type=jnp.float32) + jnp.dot(aggregate, w_neigh, preferred_element_type=jnp.float32)
    sigmoid_pre = jax.nn.sigmoid(preact)
    activations = (preact * sigmoid_pre).astype(jnp.bfloat16)
    slope = sigmoid_pre * (1.0 + preact * (1.0 - sigmoid_pre))
    dpreact = (cotangent.astype(jnp.float32) * slope).astype(jnp.bfloat16)
    grad_scale = 1.0 / math.sqrt(NODES)
    grad_self = jnp.dot(features.T, dpreact, preferred_element_type=jnp.float32) * grad_scale
    grad_neigh = jnp.dot(aggregate.T, dpreact, preferred_element_type=jnp.float32) * grad_scale
    dscaled = (jnp.dot(dpreact, w_neigh.T, preferred_element_type=jnp.float32) / degree_wide).astype(jnp.bfloat16)
    dscaled_wide = dscaled.astype(jnp.float32)

    def spread_step(running, device):
        targets, sources, in_use = device_edges(device, tile_rows, tile_cols, tile_edges, tile_count)
        update = dscaled_wide[targets] * in_use[:, None, None]
        flat_update = update.reshape(-1, F)
        for edge_number in range(EDGE_K):
            running = running.at[sources[edge_number].reshape(-1)].add(flat_update)
        return (running, None)
    neighbour_grad, _ = lax.scan(spread_step, jnp.zeros((NODES, F), jnp.float32), devices_all)
    feature_grad = (jnp.dot(dpreact, w_self.T, preferred_element_type=jnp.float32) + neighbour_grad).astype(jnp.bfloat16)
    return (activations, feature_grad, grad_self, grad_neigh)
```

```python
import functools
import math

import jax
import jax.numpy as jnp
from jax import lax
from jax.experimental import pallas as pl
from jax.experimental.pallas import tpu as pltpu
from jax.sharding import PartitionSpec as P

VMEM_LIMIT = 48 * 1024 * 1024
UNROLL = 8
UNUSED = 255


class Copies:
    def __init__(self, send_sems):
        self.send_sems = send_sems
        self.started = []

    def send(self, src, dst, recv_sem, device, cond=None):
        copy = pltpu.make_async_remote_copy(
            src_ref=src,
            dst_ref=dst,
            send_sem=self.send_sems.at[len(self.started)],
            recv_sem=recv_sem,
            device_id=device,
            device_id_type=pl.DeviceIdType.MESH,
        )
        self.started.append((cond, copy))
        if cond is None:
            copy.start()
        else:
            pl.when(cond)(lambda: copy.start())

    def wait_recv(self, dst, recv_sem, device):
        pltpu.make_async_remote_copy(
            src_ref=dst,
            dst_ref=dst,
            send_sem=self.send_sems.at[0],
            recv_sem=recv_sem,
            device_id=device,
            device_id_type=pl.DeviceIdType.MESH,
        ).wait_recv()

    def finish(self):
        for cond, copy in self.started:
            if cond is None:
                copy.wait_send()
            else:
                pl.when(cond)(lambda copy=copy: copy.wait_send())


def signal(device):
    pl.semaphore_signal(
        pltpu.get_barrier_semaphore(),
        inc=1,
        device_id=device,
        device_id_type=pl.DeviceIdType.MESH,
    )


def both(x, y):
    return jnp.logical_and(x, y)


def gather_rows_kernel(n_row, own_ref, out_ref, send_sems, recv_sems, local_sem):
    groups = n_row // 2
    half = own_ref.shape[0] // 2
    me = lax.axis_index("row")
    place = me // 2
    core = me % 2
    sibling = {"row": place * 2 + (1 - core)}
    peers = [{"row": lax.rem(place + k, groups) * 2 + core} for k in range(1, groups)]
    for device in [sibling] + peers:
        signal(device)
    keep = pltpu.make_async_copy(own_ref, out_ref.at[me], local_sem)
    keep.start()
    pl.semaphore_wait(pltpu.get_barrier_semaphore(), groups)
    copies = Copies(send_sems)
    for part in range(2):
        rows = pl.ds(part * half, half)
        for device in peers + [sibling]:
            copies.send(
                own_ref.at[rows], out_ref.at[me, rows], recv_sems.at[me, part], device
            )
    for part in range(2):
        rows = pl.ds(part * half, half)
        for k in range(1, groups):
            source = lax.rem(place + groups - k, groups) * 2 + core
            block = out_ref.at[source, rows]
            copies.wait_recv(block, recv_sems.at[source, part], sibling)
            copies.send(block, block, recv_sems.at[source, part], sibling)
    for part in range(2):
        rows = pl.ds(part * half, half)
        for k in range(groups):
            source = lax.rem(place + groups - k, groups) * 2 + (1 - core)
            copies.wait_recv(out_ref.at[source, rows], recv_sems.at[source, part], sibling)
    keep.wait()
    copies.finish()


def gather_rows(features, n_row):
    rows, width = features.shape
    return pl.pallas_call(
        functools.partial(gather_rows_kernel, n_row),
        out_shape=jax.ShapeDtypeStruct((n_row, rows, width), features.dtype),
        in_specs=[pl.BlockSpec(memory_space=pltpu.VMEM)],
        out_specs=pl.BlockSpec(memory_space=pltpu.VMEM),
        scratch_shapes=[
            pltpu.SemaphoreType.DMA((4 * n_row,)),
            pltpu.SemaphoreType.DMA((n_row, 2)),
            pltpu.SemaphoreType.DMA,
        ],
        compiler_params=pltpu.CompilerParams(
            collective_id=0, has_side_effects=True, vmem_limit_bytes=VMEM_LIMIT
        ),
        name="gather_rows",
    )(features)


def spread_kernel(
    forward, rows_ref, cols_ref, count_ref, edges_ref, nodes_ref, out_ref, acc_ref
):
    tile = edges_ref.shape[2]
    edge_count = edges_ref.shape[0]
    acc_ref[...] = jnp.zeros_like(acc_ref)
    column = (
        lax.broadcasted_iota(jnp.int32, (tile // 16, 16, tile), 0) * 16
        + lax.broadcasted_iota(jnp.int32, (tile // 16, 16, tile), 1)
    ).astype(jnp.float32).astype(jnp.bfloat16)
    one = jnp.ones(column.shape, jnp.bfloat16)
    zero = jnp.zeros(column.shape, jnp.bfloat16)

    def pattern(slot):
        total = None
        for k in range(edge_count):
            row = edges_ref[k, pl.ds(slot, 1), :]
            wide = jnp.broadcast_to(row, (16, tile)).astype(jnp.float32).astype(jnp.bfloat16)
            hit = jnp.where(wide[None] == column, one, zero)
            total = hit if total is None else total + hit
        return total.reshape(tile, tile)

    def body(step, carry):
        first = step * UNROLL
        products = []
        for u in range(UNROLL):
            slot = first + u
            if forward:
                products.append(
                    lax.dot_general(
                        pattern(slot),
                        nodes_ref[cols_ref[slot]],
                        (((0,), (0,)), ((), ())),
                        preferred_element_type=jnp.float32,
                    )
                )
            else:
                products.append(
                    jnp.dot(
                        pattern(slot),
                        nodes_ref[rows_ref[slot]],
                        preferred_element_type=jnp.float32,
                    )
                )
        for u in range(UNROLL):
            slot = first + u
            target = rows_ref[slot] if forward else cols_ref[slot]
            acc_ref[target] += products[u]
        return carry

    steps = lax.div(count_ref[0] + (UNROLL - 1), UNROLL)
    lax.fori_loop(0, steps, body, 0)

    def finish(index, carry):
        out_ref[index] = acc_ref[index].astype(out_ref.dtype)
        return carry

    lax.fori_loop(0, out_ref.shape[0], finish, 0)


def spread(forward, tile_rows, tile_cols, tile_count, edges, nodes, out_tiles):
    tile = edges.shape[2]
    width = nodes.shape[-1]
    node_tiles = nodes.reshape(-1, tile, width)
    smem = pl.BlockSpec(memory_space=pltpu.SMEM)
    vmem = pl.BlockSpec(memory_space=pltpu.VMEM)
    return pl.pallas_call(
        functools.partial(spread_kernel, forward),
        out_shape=jax.ShapeDtypeStruct((out_tiles, tile, width), jnp.bfloat16),
        in_specs=[smem, smem, smem, vmem, vmem],
        out_specs=vmem,
        scratch_shapes=[pltpu.VMEM((out_tiles, tile, width), jnp.float32)],
        compiler_params=pltpu.CompilerParams(vmem_limit_bytes=VMEM_LIMIT),
        cost_estimate=pl.CostEstimate(
            flops=2 * edges.shape[1] * tile * tile * width,
            bytes_accessed=edges.size * 4 + nodes.size * 2 + out_tiles * tile * width * 2,
            transcendentals=0,
        ),
        name="spread_forward" if forward else "spread_back",
    )(tile_rows, tile_cols, tile_count, edges, node_tiles)


def layer_kernel(
    far,
    near,
    part_ref,
    feat_ref,
    w_self_ref,
    w_neigh_ref,
    cot_ref,
    degree_ref,
    act_ref,
    own_ref,
    grads_ref,
    all_ref,
    below_a,
    above_a,
    below_b,
    above_b,
    cross_a,
    cross_b,
    stage_a,
    stage_b,
    total,
    tmp,
    agg,
    dpre,
    send_sems,
    below_a_sems,
    above_a_sems,
    below_b_sems,
    above_b_sems,
    cross_a_sems,
    cross_b_sems,
    gather_sems,
):
    f32, bf16 = jnp.float32, jnp.bfloat16
    rows, width = feat_ref.shape
    half = rows // 2
    upper, lower = pl.ds(0, half), pl.ds(half, half)
    me = lax.axis_index("col")
    a = me // near
    b = me % near

    def at(a_index, b_index):
        return {"col": a_index * near + b_index}

    has_below, has_above = a > 0, a < far - 1
    below, above = at(a - 1, b), at(a + 1, b)
    ahead = [lax.rem(b + k, near) for k in range(1, near)]
    behind = [lax.rem(b + near - k, near) for k in range(1, near)]
    any_peer = at(a, ahead[0]) if near > 1 else at(lax.rem(a + 1, far), b)

    for other in ahead:
        signal(at(a, other))
    pl.when(has_below)(lambda: signal(below))
    pl.when(has_above)(lambda: signal(above))
    greeted = near - 1 + has_below.astype(jnp.int32) + has_above.astype(jnp.int32)
    pl.semaphore_wait(pltpu.get_barrier_semaphore(), greeted)

    copies = Copies(send_sems)
    up = (1, above, has_below, below_a, below_a_sems, below_b, below_b_sems)
    down = (-1, below, has_above, above_a, above_a_sems, above_b, above_b_sems)

    def reached(index):
        return both(index >= 0, index < far)

    for d in range(far - 1, -1, -1):
        for sign in (1, -1) if d else (1,):
            dest = a + sign * d
            for k in range(1, near):
                copies.send(
                    part_ref.at[dest * near + ahead[k - 1], lower],
                    cross_b.at[k - 1, dest],
                    cross_b_sems.at[k - 1, dest],
                    at(a, ahead[k - 1]),
                    reached(dest) if d else None,
                )
    for d in range(far - 1, 0, -1):
        for sign, onward, arrives, got_a, got_a_sems, got_b, got_b_sems in (up, down):
            dest = a + sign * d
            valid = reached(dest)
            for b_index in range(near):
                j = dest * near + b_index

                @pl.when(both(valid, arrives))
                def _():
                    copies.wait_recv(got_a.at[j], got_a_sems.at[j], any_peer)
                    stage_a[j] = (
                        part_ref[j, upper].astype(f32) + got_a[j].astype(f32)
                    ).astype(bf16)

                @pl.when(both(valid, jnp.logical_not(arrives)))
                def _():
                    stage_a[j] = part_ref[j, upper]

                copies.send(stage_a.at[j], got_a.at[j], got_a_sems.at[j], onward, valid)
        for sign, onward, arrives, got_a, got_a_sems, got_b, got_b_sems in (up, down):
            dest = a + sign * d
            valid = reached(dest)

            @pl.when(valid)
            def _():
                value = part_ref[dest * near + b, lower].astype(f32)
                for k in range(1, near):
                    copies.wait_recv(
                        cross_b.at[k - 1, dest], cross_b_sems.at[k - 1, dest], any_peer
                    )
                    value = value + cross_b[k - 1, dest].astype(f32)
                tmp[...] = value

            @pl.when(both(valid, arrives))
            def _():
                copies.wait_recv(got_b.at[dest], got_b_sems.at[dest], any_peer)
                tmp[...] += got_b[dest].astype(f32)

            @pl.when(valid)
            def _():
                stage_b[dest] = tmp[...].astype(bf16)

            copies.send(stage_b.at[dest], got_b.at[dest], got_b_sems.at[dest], onward, valid)

    def add_both(ref, window, arrived_below, below_sem, arrived_above, above_sem):
        @pl.when(has_below)
        def _():
            copies.wait_recv(arrived_below, below_sem, any_peer)
            ref[window] += arrived_below[...].astype(f32)

        @pl.when(has_above)
        def _():
            copies.wait_recv(arrived_above, above_sem, any_peer)
            ref[window] += arrived_above[...].astype(f32)

    whole = pl.ds(0, half)
    for k in range(1, near):
        j = a * near + ahead[k - 1]
        tmp[...] = part_ref[j, upper].astype(f32)
        add_both(tmp, whole, below_a.at[j], below_a_sems.at[j], above_a.at[j], above_a_sems.at[j])
        stage_a[j] = tmp[...].astype(bf16)
        copies.send(
            stage_a.at[j], cross_a.at[k - 1], cross_a_sems.at[k - 1], at(a, ahead[k - 1])
        )
    total[upper] = part_ref[me, upper].astype(f32)
    add_both(
        total, upper, below_a.at[me], below_a_sems.at[me], above_a.at[me], above_a_sems.at[me]
    )
    total[lower] = part_ref[me, lower].astype(f32)
    for k in range(1, near):
        copies.wait_recv(cross_b.at[k - 1, a], cross_b_sems.at[k - 1, a], any_peer)
        total[lower] += cross_b[k - 1, a].astype(f32)
    add_both(
        total, lower, below_b.at[a], below_b_sems.at[a], above_b.at[a], above_b_sems.at[a]
    )

    def layer(window):
        degree = degree_ref[window]
        aggregate = (total[window] / degree).astype(bf16)
        agg[window] = aggregate
        preact = jnp.dot(
            feat_ref[window], w_self_ref[...], preferred_element_type=f32
        ) + jnp.dot(aggregate, w_neigh_ref[...], preferred_element_type=f32)
        gate = jax.nn.sigmoid(preact)
        act_ref[window] = (preact * gate).astype(bf16)
        slope = gate * (1.0 + preact * (1.0 - gate))
        dpreact = (cot_ref[window].astype(f32) * slope).astype(bf16)
        dpre[window] = dpreact
        back = lax.dot_general(
            dpreact, w_neigh_ref[...], (((1,), (1,)), ((), ())), preferred_element_type=f32
        )
        all_ref[me, window] = (back / degree).astype(bf16)

    def hand_on(j, window, part, device, cond=None):
        copies.send(
            all_ref.at[j, window], all_ref.at[j, window], gather_sems.at[part, j], device, cond
        )

    def arrive(j, window, part):
        copies.wait_recv(all_ref.at[j, window], gather_sems.at[part, j], any_peer)

    layer(lower)
    hand_on(me, lower, 1, above, has_above)
    hand_on(me, lower, 1, below, has_below)
    for other in ahead:
        hand_on(me, lower, 1, at(a, other))
    for k in range(1, near):
        copies.wait_recv(cross_a.at[k - 1], cross_a_sems.at[k - 1], any_peer)
        total[upper] += cross_a[k - 1].astype(f32)
    layer(upper)
    for other in ahead:
        hand_on(me, upper, 0, at(a, other))
    hand_on(me, upper, 0, above, has_above)
    hand_on(me, upper, 0, below, has_below)

    contract_rows = (((0,), (0,)), ((), ()))
    grads_ref[0] = lax.dot_general(
        feat_ref[...], dpre[...], contract_rows, preferred_element_type=f32
    )
    grads_ref[1] = lax.dot_general(
        agg[...], dpre[...], contract_rows, preferred_element_type=f32
    )
    for other in behind:
        j = a * near + other
        arrive(j, upper, 0)
        hand_on(j, upper, 0, above, has_above)
        hand_on(j, upper, 0, below, has_below)
    own_ref[...] = lax.dot_general(
        dpre[...], w_self_ref[...], (((1,), (1,)), ((), ())), preferred_element_type=f32
    )
    sides = ((1, above, has_above), (-1, below, has_below))
    for d in range(1, far):
        for sign, onward, goes_on in sides:
            source = a - sign * d
            valid = reached(source)
            j = source * near + b
            pl.when(valid)(lambda: arrive(j, lower, 1))
            hand_on(j, lower, 1, onward, both(valid, goes_on))
            for other in ahead:
                hand_on(j, lower, 1, at(a, other), valid)
        for sign, onward, goes_on in sides:
            source = a - sign * d
            valid = reached(source)
            for b_index in range(near):
                j = source * near + b_index
                pl.when(valid)(lambda: arrive(j, upper, 0))
                hand_on(j, upper, 0, onward, both(valid, goes_on))
    for a_index in range(far):
        for other in behind:
            arrive(a_index * near + other, lower, 1)
    copies.finish()


def layer_call(partials, features, w_self, w_neigh, cotangent, degree, n_col):
    far = 4 if n_col % 4 == 0 else n_col
    near = n_col // far
    rows, width = features.shape
    half = rows // 2
    bf16, f32 = jnp.bfloat16, jnp.float32
    vmem = pl.BlockSpec(memory_space=pltpu.VMEM)
    crosses = max(near - 1, 1)
    dma = pltpu.SemaphoreType.DMA
    return pl.pallas_call(
        functools.partial(layer_kernel, far, near),
        out_shape=(
            jax.ShapeDtypeStruct((rows, width), bf16),
            jax.ShapeDtypeStruct((rows, width), f32),
            jax.ShapeDtypeStruct((2, width, width), f32),
            jax.ShapeDtypeStruct((n_col, rows, width), bf16),
        ),
        in_specs=[vmem] * 6,
        out_specs=(vmem,) * 4,
        scratch_shapes=[
            pltpu.VMEM((n_col, half, width), bf16),
            pltpu.VMEM((n_col, half, width), bf16),
            pltpu.VMEM((far, half, width), bf16),
            pltpu.VMEM((far, half, width), bf16),
            pltpu.VMEM((crosses, half, width), bf16),
            pltpu.VMEM((crosses, far, half, width), bf16),
            pltpu.VMEM((n_col, half, width), bf16),
            pltpu.VMEM((far, half, width), bf16),
            pltpu.VMEM((rows, width), f32),
            pltpu.VMEM((half, width), f32),
            pltpu.VMEM((rows, width), bf16),
            pltpu.VMEM((rows, width), bf16),
            dma((16 * n_col,)),
            dma((n_col,)),
            dma((n_col,)),
            dma((far,)),
            dma((far,)),
            dma((crosses,)),
            dma((crosses, far)),
            dma((2, n_col)),
        ],
        compiler_params=pltpu.CompilerParams(
            collective_id=1, has_side_effects=True, vmem_limit_bytes=VMEM_LIMIT
        ),
        name="layer",
    )(partials, features, w_self, w_neigh, cotangent, degree)


def scatter_rows_kernel(
    n_row, part_ref, own_ref, out_ref, from_sibling, staged, from_peer, total, send_sems,
    sibling_sems, peer_sems,
):
    f32 = jnp.float32
    groups = n_row // 2
    half = own_ref.shape[0] // 2
    me = lax.axis_index("row")
    place = me // 2
    core = me % 2
    sibling = {"row": place * 2 + (1 - core)}
    peers = [lax.rem(place + k, groups) for k in range(1, groups)]
    for device in [sibling] + [{"row": peer * 2 + core} for peer in peers]:
        signal(device)
    pl.semaphore_wait(pltpu.get_barrier_semaphore(), groups)
    copies = Copies(send_sems)
    windows = [pl.ds(part * half, half) for part in range(2)]
    for peer in peers + [place]:
        for part, rows in enumerate(windows):
            copies.send(
                part_ref.at[peer * 2 + (1 - core), rows],
                from_sibling.at[peer, rows],
                sibling_sems.at[peer, part],
                sibling,
            )
    for k, peer in enumerate(peers):
        for part, rows in enumerate(windows):
            copies.wait_recv(from_sibling.at[peer, rows], sibling_sems.at[peer, part], sibling)
            staged[k, rows] = (
                part_ref[peer * 2 + core, rows].astype(f32)
                + from_sibling[peer, rows].astype(f32)
            ).astype(staged.dtype)
            copies.send(
                staged.at[k, rows],
                from_peer.at[k, rows],
                peer_sems.at[k, part],
                {"row": peer * 2 + core},
            )
    for part, rows in enumerate(windows):
        copies.wait_recv(from_sibling.at[place, rows], sibling_sems.at[place, part], sibling)
        total[rows] = (
            own_ref[rows]
            + part_ref[me, rows].astype(f32)
            + from_sibling[place, rows].astype(f32)
        )
    for part, rows in enumerate(windows):
        value = total[rows]
        for k in range(groups - 1):
            copies.wait_recv(from_peer.at[k, rows], peer_sems.at[k, part], sibling)
            value = value + from_peer[k, rows].astype(f32)
        out_ref[rows] = value.astype(out_ref.dtype)
    copies.finish()


def scatter_rows(partials, own_grad, n_row):
    rows, width = own_grad.shape
    groups = n_row // 2
    others = max(groups - 1, 1)
    vmem = pl.BlockSpec(memory_space=pltpu.VMEM)
    bf16 = jnp.bfloat16
    dma = pltpu.SemaphoreType.DMA
    return pl.pallas_call(
        functools.partial(scatter_rows_kernel, n_row),
        out_shape=jax.ShapeDtypeStruct((rows, width), bf16),
        in_specs=[vmem] * 2,
        out_specs=vmem,
        scratch_shapes=[
            pltpu.VMEM((groups, rows, width), bf16),
            pltpu.VMEM((others, rows, width), bf16),
            pltpu.VMEM((others, rows, width), bf16),
            pltpu.VMEM((rows, width), jnp.float32),
            dma((4 * groups,)),
            dma((groups, 2)),
            dma((others, 2)),
        ],
        compiler_params=pltpu.CompilerParams(
            collective_id=2, has_side_effects=True, vmem_limit_bytes=VMEM_LIMIT
        ),
        name="scatter_rows",
    )(partials, own_grad)


def per_device(
    features, w_self, w_neigh, cotangent, degree, tile_rows, tile_cols, tile_edges, tile_count
):
    rows, width = features.shape
    tile = tile_edges.shape[2]
    slots = tile_rows.shape[0]
    n_row = lax.axis_size("row")
    n_col = lax.axis_size("col")
    in_use = jnp.arange(slots, dtype=jnp.int32) < tile_count[0]
    edges = jnp.where(in_use[None, :, None], tile_edges, UNUSED)
    padding = (-slots) % UNROLL
    if padding:
        edges = jnp.pad(edges, ((0, 0), (0, padding), (0, 0)), constant_values=UNUSED)
        tile_rows = jnp.pad(tile_rows, (0, padding))
        tile_cols = jnp.pad(tile_cols, (0, padding))
    degree_wide = degree.astype(jnp.float32)[:, None]

    column_nodes = gather_rows(features, n_row)
    partial_sums = spread(
        True, tile_rows, tile_cols, tile_count, edges, column_nodes, rows * n_col // tile
    )
    activations, own_grad, grads, row_nodes = layer_call(
        partial_sums.reshape(n_col, rows, width),
        features,
        w_self,
        w_neigh,
        cotangent,
        degree_wide,
        n_col,
    )
    partial_grads = spread(
        False, tile_rows, tile_cols, tile_count, edges, row_nodes, rows * n_row // tile
    )
    grads = lax.psum(grads, ("row", "col")) * (1.0 / math.sqrt(rows * n_row * n_col))
    feature_grad = scatter_rows(partial_grads.reshape(n_row, rows, width), own_grad, n_row)
    return (activations, feature_grad, grads[0], grads[1])


def solution(mesh):
    nodes = P(("row", "col"), None)
    flat = P(("row", "col"))
    return jax.shard_map(
        per_device,
        mesh=mesh,
        in_specs=(nodes, P(), P(), nodes, flat, flat, flat, P(None, ("row", "col"), None), flat),
        out_specs=(nodes, nodes, P(), P()),
        check_vma=False,
    )
```

```python
import functools
import math

import jax
import jax.numpy as jnp
from jax import lax
from jax.experimental import pallas as pl
from jax.experimental.pallas import tpu as pltpu
from jax.sharding import PartitionSpec as P

VMEM_LIMIT = 48 * 1024 * 1024
UNROLL = 8
UNUSED = 255


class Copies:
    def __init__(self, send_sems):
        self.send_sems = send_sems
        self.started = []

    def send(self, src, dst, recv_sem, device, cond=None):
        copy = pltpu.make_async_remote_copy(
            src_ref=src,
            dst_ref=dst,
            send_sem=self.send_sems.at[len(self.started)],
            recv_sem=recv_sem,
            device_id=device,
            device_id_type=pl.DeviceIdType.MESH,
        )
        self.started.append((cond, copy))
        if cond is None:
            copy.start()
        else:
            pl.when(cond)(lambda: copy.start())

    def wait_recv(self, dst, recv_sem, device):
        pltpu.make_async_remote_copy(
            src_ref=dst,
            dst_ref=dst,
            send_sem=self.send_sems.at[0],
            recv_sem=recv_sem,
            device_id=device,
            device_id_type=pl.DeviceIdType.MESH,
        ).wait_recv()

    def finish(self):
        for cond, copy in self.started:
            if cond is None:
                copy.wait_send()
            else:
                pl.when(cond)(lambda copy=copy: copy.wait_send())


def signal(device):
    pl.semaphore_signal(
        pltpu.get_barrier_semaphore(),
        inc=1,
        device_id=device,
        device_id_type=pl.DeviceIdType.MESH,
    )


def both(x, y):
    return jnp.logical_and(x, y)


def gather_rows_kernel(n_row, own_ref, out_ref, send_sems, recv_sems, local_sem):
    groups = n_row // 2
    half = own_ref.shape[0] // 2
    me = lax.axis_index("row")
    place = me // 2
    core = me % 2
    sibling = {"row": place * 2 + (1 - core)}
    peers = [{"row": lax.rem(place + k, groups) * 2 + core} for k in range(1, groups)]
    for device in [sibling] + peers:
        signal(device)
    keep = pltpu.make_async_copy(own_ref, out_ref.at[me], local_sem)
    keep.start()
    pl.semaphore_wait(pltpu.get_barrier_semaphore(), groups)
    copies = Copies(send_sems)
    for part in range(2):
        rows = pl.ds(part * half, half)
        for device in peers + [sibling]:
            copies.send(
                own_ref.at[rows], out_ref.at[me, rows], recv_sems.at[me, part], device
            )
    for part in range(2):
        rows = pl.ds(part * half, half)
        for k in range(1, groups):
            source = lax.rem(place + groups - k, groups) * 2 + core
            block = out_ref.at[source, rows]
            copies.wait_recv(block, recv_sems.at[source, part], sibling)
            copies.send(block, block, recv_sems.at[source, part], sibling)
    for part in range(2):
        rows = pl.ds(part * half, half)
        for k in range(groups):
            source = lax.rem(place + groups - k, groups) * 2 + (1 - core)
            copies.wait_recv(out_ref.at[source, rows], recv_sems.at[source, part], sibling)
    keep.wait()
    copies.finish()


def gather_rows(features, n_row):
    rows, width = features.shape
    return pl.pallas_call(
        functools.partial(gather_rows_kernel, n_row),
        out_shape=jax.ShapeDtypeStruct((n_row, rows, width), features.dtype),
        in_specs=[pl.BlockSpec(memory_space=pltpu.VMEM)],
        out_specs=pl.BlockSpec(memory_space=pltpu.VMEM),
        scratch_shapes=[
            pltpu.SemaphoreType.DMA((4 * n_row,)),
            pltpu.SemaphoreType.DMA((n_row, 2)),
            pltpu.SemaphoreType.DMA,
        ],
        compiler_params=pltpu.CompilerParams(
            collective_id=0, has_side_effects=True, vmem_limit_bytes=VMEM_LIMIT
        ),
        name="gather_rows",
    )(features)


def spread_kernel(
    forward, rows_ref, cols_ref, count_ref, edges_ref, nodes_ref, out_ref, acc_ref
):
    tile = edges_ref.shape[2]
    edge_count = edges_ref.shape[0]
    acc_ref[...] = jnp.zeros_like(acc_ref)
    column = (
        lax.broadcasted_iota(jnp.int32, (tile // 16, 16, tile), 0) * 16
        + lax.broadcasted_iota(jnp.int32, (tile // 16, 16, tile), 1)
    ).astype(jnp.float32).astype(jnp.bfloat16)
    one = jnp.ones(column.shape, jnp.bfloat16)
    zero = jnp.zeros(column.shape, jnp.bfloat16)

    def pattern(slot):
        total = None
        for k in range(edge_count):
            row = edges_ref[k, pl.ds(slot, 1), :]
            wide = jnp.broadcast_to(row, (16, tile)).astype(jnp.float32).astype(jnp.bfloat16)
            hit = jnp.where(wide[None] == column, one, zero)
            total = hit if total is None else total + hit
        return total.reshape(tile, tile)

    def body(step, carry):
        first = step * UNROLL
        products = []
        for u in range(UNROLL):
            slot = first + u
            if forward:
                products.append(
                    lax.dot_general(
                        pattern(slot),
                        nodes_ref[cols_ref[slot]],
                        (((0,), (0,)), ((), ())),
                        preferred_element_type=jnp.float32,
                    )
                )
            else:
                products.append(
                    jnp.dot(
                        pattern(slot),
                        nodes_ref[rows_ref[slot]],
                        preferred_element_type=jnp.float32,
                    )
                )
        for u in range(UNROLL):
            slot = first + u
            target = rows_ref[slot] if forward else cols_ref[slot]
            acc_ref[target] += products[u]
        return carry

    steps = lax.div(count_ref[0] + (UNROLL - 1), UNROLL)
    lax.fori_loop(0, steps, body, 0)

    def finish(index, carry):
        out_ref[index] = acc_ref[index].astype(out_ref.dtype)
        return carry

    lax.fori_loop(0, out_ref.shape[0], finish, 0)


def spread(forward, tile_rows, tile_cols, tile_count, edges, nodes, out_tiles):
    tile = edges.shape[2]
    width = nodes.shape[-1]
    node_tiles = nodes.reshape(-1, tile, width)
    smem = pl.BlockSpec(memory_space=pltpu.SMEM)
    vmem = pl.BlockSpec(memory_space=pltpu.VMEM)
    return pl.pallas_call(
        functools.partial(spread_kernel, forward),
        out_shape=jax.ShapeDtypeStruct((out_tiles, tile, width), jnp.bfloat16),
        in_specs=[smem, smem, smem, vmem, vmem],
        out_specs=vmem,
        scratch_shapes=[pltpu.VMEM((out_tiles, tile, width), jnp.float32)],
        compiler_params=pltpu.CompilerParams(vmem_limit_bytes=VMEM_LIMIT),
        cost_estimate=pl.CostEstimate(
            flops=2 * edges.shape[1] * tile * tile * width,
            bytes_accessed=edges.size * 4 + nodes.size * 2 + out_tiles * tile * width * 2,
            transcendentals=0,
        ),
        name="spread_forward" if forward else "spread_back",
    )(tile_rows, tile_cols, tile_count, edges, node_tiles)


def split_rows(rows):
    first_rows = rows * 3 // 16
    return first_rows, (rows - first_rows) // 2


def layer_kernel(
    far,
    near,
    part_ref,
    feat_ref,
    w_self_ref,
    w_neigh_ref,
    cot_ref,
    degree_ref,
    act_ref,
    own_ref,
    grads_ref,
    all_ref,
    below_a,
    above_a,
    below_b,
    above_b,
    cross_a,
    cross_b,
    stage_a,
    stage_b,
    total,
    tmp,
    agg,
    dpre,
    send_sems,
    below_a_sems,
    above_a_sems,
    below_b_sems,
    above_b_sems,
    cross_a_sems,
    cross_b_sems,
    gather_sems,
):
    f32, bf16 = jnp.float32, jnp.bfloat16
    rows, width = feat_ref.shape
    first_rows, piece_rows = split_rows(rows)
    first = pl.ds(0, first_rows)
    pieces = [pl.ds(start, piece_rows) for start in range(first_rows, rows, piece_rows)]
    me = lax.axis_index("col")
    a = me // near
    b = me % near

    def at(a_index, b_index):
        return {"col": a_index * near + b_index}

    has_below, has_above = a > 0, a < far - 1
    below, above = at(a - 1, b), at(a + 1, b)
    ahead = [lax.rem(b + k, near) for k in range(1, near)]
    behind = [lax.rem(b + near - k, near) for k in range(1, near)]
    any_peer = at(a, ahead[0]) if near > 1 else at(lax.rem(a + 1, far), b)

    for other in ahead:
        signal(at(a, other))
    pl.when(has_below)(lambda: signal(below))
    pl.when(has_above)(lambda: signal(above))
    greeted = near - 1 + has_below.astype(jnp.int32) + has_above.astype(jnp.int32)
    pl.semaphore_wait(pltpu.get_barrier_semaphore(), greeted)

    copies = Copies(send_sems)
    up = (1, above, has_below, below_a, below_a_sems, below_b, below_b_sems)
    down = (-1, below, has_above, above_a, above_a_sems, above_b, above_b_sems)

    def reached(index):
        return both(index >= 0, index < far)

    for d in range(far - 1, -1, -1):
        for sign in (1, -1) if d else (1,):
            dest = a + sign * d
            for piece, window in enumerate(pieces):
                for k in range(1, near):
                    copies.send(
                        part_ref.at[dest * near + ahead[k - 1], window],
                        cross_b.at[k - 1, dest, piece],
                        cross_b_sems.at[k - 1, dest, piece],
                        at(a, ahead[k - 1]),
                        reached(dest) if d else None,
                    )
    for d in range(far - 1, 0, -1):
        for sign, onward, arrives, got_a, got_a_sems, got_b, got_b_sems in (up, down):
            dest = a + sign * d
            valid = reached(dest)
            for b_index in range(near):
                j = dest * near + b_index

                @pl.when(both(valid, arrives))
                def _():
                    copies.wait_recv(got_a.at[j], got_a_sems.at[j], any_peer)
                    stage_a[j] = (
                        part_ref[j, first].astype(f32) + got_a[j].astype(f32)
                    ).astype(bf16)

                @pl.when(both(valid, jnp.logical_not(arrives)))
                def _():
                    stage_a[j] = part_ref[j, first]

                copies.send(stage_a.at[j], got_a.at[j], got_a_sems.at[j], onward, valid)
        for piece, window in enumerate(pieces):
            for sign, onward, arrives, got_a, got_a_sems, got_b, got_b_sems in (up, down):
                dest = a + sign * d
                valid = reached(dest)

                @pl.when(valid)
                def _():
                    value = part_ref[dest * near + b, window].astype(f32)
                    for k in range(1, near):
                        copies.wait_recv(
                            cross_b.at[k - 1, dest, piece],
                            cross_b_sems.at[k - 1, dest, piece],
                            any_peer,
                        )
                        value = value + cross_b[k - 1, dest, piece].astype(f32)
                    tmp[...] = value

                @pl.when(both(valid, arrives))
                def _():
                    copies.wait_recv(got_b.at[dest, piece], got_b_sems.at[dest, piece], any_peer)
                    tmp[...] += got_b[dest, piece].astype(f32)

                @pl.when(valid)
                def _():
                    stage_b[dest, piece] = tmp[...].astype(bf16)

                copies.send(
                    stage_b.at[dest, piece],
                    got_b.at[dest, piece],
                    got_b_sems.at[dest, piece],
                    onward,
                    valid,
                )

    def add_both(ref, window, arrived_below, below_sem, arrived_above, above_sem):
        @pl.when(has_below)
        def _():
            copies.wait_recv(arrived_below, below_sem, any_peer)
            ref[window] += arrived_below[...].astype(f32)

        @pl.when(has_above)
        def _():
            copies.wait_recv(arrived_above, above_sem, any_peer)
            ref[window] += arrived_above[...].astype(f32)

    lead = pl.ds(0, first_rows)
    for k in range(1, near):
        j = a * near + ahead[k - 1]
        tmp[lead] = part_ref[j, first].astype(f32)
        add_both(tmp, lead, below_a.at[j], below_a_sems.at[j], above_a.at[j], above_a_sems.at[j])
        stage_a[j] = tmp[lead].astype(bf16)
        copies.send(
            stage_a.at[j], cross_a.at[k - 1], cross_a_sems.at[k - 1], at(a, ahead[k - 1])
        )

    def layer(window):
        degree = degree_ref[window]
        aggregate = (total[window] / degree).astype(bf16)
        agg[window] = aggregate
        preact = jnp.dot(
            feat_ref[window], w_self_ref[...], preferred_element_type=f32
        ) + jnp.dot(aggregate, w_neigh_ref[...], preferred_element_type=f32)
        gate = jax.nn.sigmoid(preact)
        act_ref[window] = (preact * gate).astype(bf16)
        slope = gate * (1.0 + preact * (1.0 - gate))
        dpreact = (cot_ref[window].astype(f32) * slope).astype(bf16)
        dpre[window] = dpreact
        back = lax.dot_general(
            dpreact, w_neigh_ref[...], (((1,), (1,)), ((), ())), preferred_element_type=f32
        )
        all_ref[me, window] = (back / degree).astype(bf16)

    def hand_on(j, window, part, device, cond=None):
        copies.send(
            all_ref.at[j, window], all_ref.at[j, window], gather_sems.at[part, j], device, cond
        )

    def arrive(j, window, part):
        copies.wait_recv(all_ref.at[j, window], gather_sems.at[part, j], any_peer)

    for piece, window in enumerate(pieces):
        total[window] = part_ref[me, window].astype(f32)
        for k in range(1, near):
            copies.wait_recv(
                cross_b.at[k - 1, a, piece], cross_b_sems.at[k - 1, a, piece], any_peer
            )
            total[window] += cross_b[k - 1, a, piece].astype(f32)
        add_both(
            total,
            window,
            below_b.at[a, piece],
            below_b_sems.at[a, piece],
            above_b.at[a, piece],
            above_b_sems.at[a, piece],
        )
        layer(window)
        hand_on(me, window, piece, above, has_above)
        hand_on(me, window, piece, below, has_below)
        for other in ahead:
            hand_on(me, window, piece, at(a, other))
    total[first] = part_ref[me, first].astype(f32)
    add_both(
        total, first, below_a.at[me], below_a_sems.at[me], above_a.at[me], above_a_sems.at[me]
    )
    for k in range(1, near):
        copies.wait_recv(cross_a.at[k - 1], cross_a_sems.at[k - 1], any_peer)
        total[first] += cross_a[k - 1].astype(f32)
    layer(first)
    last = len(pieces)
    for other in ahead:
        hand_on(me, first, last, at(a, other))
    hand_on(me, first, last, above, has_above)
    hand_on(me, first, last, below, has_below)

    contract_rows = (((0,), (0,)), ((), ()))

    def own_grad():
        own_ref[...] = lax.dot_general(
            dpre[...], w_self_ref[...], (((1,), (1,)), ((), ())), preferred_element_type=f32
        )

    def grad_self():
        grads_ref[0] = lax.dot_general(
            feat_ref[...], dpre[...], contract_rows, preferred_element_type=f32
        )

    def grad_neigh():
        grads_ref[1] = lax.dot_general(
            agg[...], dpre[...], contract_rows, preferred_element_type=f32
        )

    beside = [own_grad, grad_self, grad_neigh]
    beside.pop(0)()
    sides = ((1, above, has_above), (-1, below, has_below))
    for d in range(far):
        if d:
            for piece, window in enumerate(pieces):
                for sign, onward, goes_on in sides:
                    source = a - sign * d
                    valid = reached(source)
                    j = source * near + b
                    pl.when(valid)(lambda: arrive(j, window, piece))
                    hand_on(j, window, piece, onward, both(valid, goes_on))
                    for other in ahead:
                        hand_on(j, window, piece, at(a, other), valid)
            for sign, onward, goes_on in sides:
                source = a - sign * d
                valid = reached(source)
                for b_index in range(near):
                    j = source * near + b_index
                    pl.when(valid)(lambda: arrive(j, first, last))
                    hand_on(j, first, last, onward, both(valid, goes_on))
        else:
            for other in behind:
                j = a * near + other
                arrive(j, first, last)
                hand_on(j, first, last, above, has_above)
                hand_on(j, first, last, below, has_below)
        if beside:
            beside.pop(0)()
    for step in beside:
        step()
    for a_index in range(far):
        for other in behind:
            for piece, window in enumerate(pieces):
                arrive(a_index * near + other, window, piece)
    copies.finish()


def layer_call(partials, features, w_self, w_neigh, cotangent, degree, n_col):
    far = 4 if n_col % 4 == 0 else n_col
    near = n_col // far
    rows, width = features.shape
    first_rows, piece_rows = split_rows(rows)
    bf16, f32 = jnp.bfloat16, jnp.float32
    vmem = pl.BlockSpec(memory_space=pltpu.VMEM)
    crosses = max(near - 1, 1)
    dma = pltpu.SemaphoreType.DMA
    return pl.pallas_call(
        functools.partial(layer_kernel, far, near),
        out_shape=(
            jax.ShapeDtypeStruct((rows, width), bf16),
            jax.ShapeDtypeStruct((rows, width), f32),
            jax.ShapeDtypeStruct((2, width, width), f32),
            jax.ShapeDtypeStruct((n_col, rows, width), bf16),
        ),
        in_specs=[vmem] * 6,
        out_specs=(vmem,) * 4,
        scratch_shapes=[
            pltpu.VMEM((n_col, first_rows, width), bf16),
            pltpu.VMEM((n_col, first_rows, width), bf16),
            pltpu.VMEM((far, 2, piece_rows, width), bf16),
            pltpu.VMEM((far, 2, piece_rows, width), bf16),
            pltpu.VMEM((crosses, first_rows, width), bf16),
            pltpu.VMEM((crosses, far, 2, piece_rows, width), bf16),
            pltpu.VMEM((n_col, first_rows, width), bf16),
            pltpu.VMEM((far, 2, piece_rows, width), bf16),
            pltpu.VMEM((rows, width), f32),
            pltpu.VMEM((piece_rows, width), f32),
            pltpu.VMEM((rows, width), bf16),
            pltpu.VMEM((rows, width), bf16),
            dma((24 * n_col,)),
            dma((n_col,)),
            dma((n_col,)),
            dma((far, 2)),
            dma((far, 2)),
            dma((crosses,)),
            dma((crosses, far, 2)),
            dma((3, n_col)),
        ],
        compiler_params=pltpu.CompilerParams(
            collective_id=1, has_side_effects=True, vmem_limit_bytes=VMEM_LIMIT
        ),
        name="layer",
    )(partials, features, w_self, w_neigh, cotangent, degree)


def scatter_rows_kernel(
    n_row,
    n_col,
    scale,
    part_ref,
    own_ref,
    grads_ref,
    out_ref,
    grad_self_ref,
    grad_neigh_ref,
    from_sibling,
    staged,
    from_peer,
    total,
    grad_parts,
    grad_cols,
    grad_rows,
    grad_all,
    send_sems,
    sibling_sems,
    peer_sems,
    grad_col_sems,
    grad_row_sems,
    grad_all_sems,
):
    f32 = jnp.float32
    chunk = grad_parts.shape[1]
    column = lax.axis_index("col")
    far_cols = [lax.rem(column + k, n_col) for k in range(1, n_col)]
    groups = n_row // 2
    half = own_ref.shape[0] // 2
    width = own_ref.shape[1]
    me = lax.axis_index("row")
    place = me // 2
    core = me % 2
    sibling = {"row": place * 2 + (1 - core)}
    peers = [lax.rem(place + k, groups) for k in range(1, groups)]
    all_rows = [lax.rem(me + k, n_row) for k in range(1, n_row)]
    for other in all_rows:
        signal({"row": other})
    for other in far_cols:
        signal({"col": other})
    shares = width // chunk
    for j in range(n_col):
        grad_parts[j] = grads_ref[
            j // shares, pl.ds(j % shares * chunk, chunk)
        ].astype(grad_parts.dtype)
    pl.semaphore_wait(pltpu.get_barrier_semaphore(), n_row - 1 + n_col - 1)
    copies = Copies(send_sems)
    for k, other in enumerate(far_cols):
        copies.send(grad_parts.at[other], grad_cols.at[k], grad_col_sems.at[k], {"col": other})
    windows = [pl.ds(part * half, half) for part in range(2)]
    for peer in peers + [place]:
        for part, rows in enumerate(windows):
            copies.send(
                part_ref.at[peer * 2 + (1 - core), rows],
                from_sibling.at[peer, rows],
                sibling_sems.at[peer, part],
                sibling,
            )
    for k, peer in enumerate(peers):
        for part, rows in enumerate(windows):
            copies.wait_recv(from_sibling.at[peer, rows], sibling_sems.at[peer, part], sibling)
            staged[k, rows] = (
                part_ref[peer * 2 + core, rows].astype(f32)
                + from_sibling[peer, rows].astype(f32)
            ).astype(staged.dtype)
            copies.send(
                staged.at[k, rows],
                from_peer.at[k, rows],
                peer_sems.at[k, part],
                {"row": peer * 2 + core},
            )
    share = grad_parts[column].astype(f32)
    for k in range(n_col - 1):
        copies.wait_recv(grad_cols.at[k], grad_col_sems.at[k], sibling)
        share = share + grad_cols[k].astype(f32)
    grad_rows[me] = share
    for other in all_rows:
        copies.send(grad_rows.at[me], grad_rows.at[me], grad_row_sems.at[me], {"row": other})
    for part, rows in enumerate(windows):
        copies.wait_recv(from_sibling.at[place, rows], sibling_sems.at[place, part], sibling)
        total[rows] = (
            own_ref[rows]
            + part_ref[me, rows].astype(f32)
            + from_sibling[place, rows].astype(f32)
        )
    for other in all_rows:
        copies.wait_recv(grad_rows.at[other], grad_row_sems.at[other], sibling)
    share = grad_rows[0]
    for index in range(1, n_row):
        share = share + grad_rows[index]
    grad_all[column] = (share * scale).astype(grad_all.dtype)
    for other in far_cols:
        copies.send(
            grad_all.at[column], grad_all.at[column], grad_all_sems.at[column], {"col": other}
        )
    for part, rows in enumerate(windows):
        value = total[rows]
        for k in range(groups - 1):
            copies.wait_recv(from_peer.at[k, rows], peer_sems.at[k, part], sibling)
            value = value + from_peer[k, rows].astype(f32)
        out_ref[rows] = value.astype(out_ref.dtype)
    for other in far_cols:
        copies.wait_recv(grad_all.at[other], grad_all_sems.at[other], sibling)
    for j in range(n_col):
        ref = (grad_self_ref, grad_neigh_ref)[j // shares]
        ref[pl.ds(j % shares * chunk, chunk)] = grad_all[j].astype(f32)
    copies.finish()


def scatter_rows(partials, own_grad, grads, n_row, n_col, scale):
    rows, width = own_grad.shape
    groups = n_row // 2
    others = max(groups - 1, 1)
    chunk = 2 * width // n_col
    vmem = pl.BlockSpec(memory_space=pltpu.VMEM)
    bf16 = jnp.bfloat16
    dma = pltpu.SemaphoreType.DMA
    return pl.pallas_call(
        functools.partial(scatter_rows_kernel, n_row, n_col, scale),
        out_shape=(
            jax.ShapeDtypeStruct((rows, width), bf16),
            jax.ShapeDtypeStruct((width, width), jnp.float32),
            jax.ShapeDtypeStruct((width, width), jnp.float32),
        ),
        in_specs=[vmem] * 3,
        out_specs=(vmem,) * 3,
        scratch_shapes=[
            pltpu.VMEM((groups, rows, width), bf16),
            pltpu.VMEM((others, rows, width), bf16),
            pltpu.VMEM((others, rows, width), bf16),
            pltpu.VMEM((rows, width), jnp.float32),
            pltpu.VMEM((n_col, chunk, width), bf16),
            pltpu.VMEM((n_col - 1, chunk, width), bf16),
            pltpu.VMEM((n_row, chunk, width), jnp.float32),
            pltpu.VMEM((n_col, chunk, width), bf16),
            dma((4 * groups + 2 * n_col + n_row,)),
            dma((groups, 2)),
            dma((others, 2)),
            dma((n_col - 1,)),
            dma((n_row,)),
            dma((n_col,)),
        ],
        compiler_params=pltpu.CompilerParams(
            collective_id=2, has_side_effects=True, vmem_limit_bytes=VMEM_LIMIT
        ),
        name="scatter_rows",
    )(partials, own_grad, grads)


def per_device(
    features, w_self, w_neigh, cotangent, degree, tile_rows, tile_cols, tile_edges, tile_count
):
    rows, width = features.shape
    tile = tile_edges.shape[2]
    slots = tile_rows.shape[0]
    n_row = lax.axis_size("row")
    n_col = lax.axis_size("col")
    in_use = jnp.arange(slots, dtype=jnp.int32) < tile_count[0]
    edges = jnp.where(in_use[None, :, None], tile_edges, UNUSED)
    padding = (-slots) % UNROLL
    if padding:
        edges = jnp.pad(edges, ((0, 0), (0, padding), (0, 0)), constant_values=UNUSED)
        tile_rows = jnp.pad(tile_rows, (0, padding))
        tile_cols = jnp.pad(tile_cols, (0, padding))
    degree_wide = degree.astype(jnp.float32)[:, None]

    column_nodes = gather_rows(features, n_row)
    partial_sums = spread(
        True, tile_rows, tile_cols, tile_count, edges, column_nodes, rows * n_col // tile
    )
    activations, own_grad, grads, row_nodes = layer_call(
        partial_sums.reshape(n_col, rows, width),
        features,
        w_self,
        w_neigh,
        cotangent,
        degree_wide,
        n_col,
    )
    partial_grads = spread(
        False, tile_rows, tile_cols, tile_count, edges, row_nodes, rows * n_row // tile
    )
    scale = 1.0 / math.sqrt(rows * n_row * n_col)
    feature_grad, grad_self, grad_neigh = scatter_rows(
        partial_grads.reshape(n_row, rows, width), own_grad, grads, n_row, n_col, scale
    )
    return (activations, feature_grad, grad_self, grad_neigh)


def solution(mesh):
    nodes = P(("row", "col"), None)
    flat = P(("row", "col"))
    return jax.shard_map(
        per_device,
        mesh=mesh,
        in_specs=(nodes, P(), P(), nodes, flat, flat, flat, P(None, ("row", "col"), None), flat),
        out_specs=(nodes, nodes, P(), P()),
        check_vma=False,
    )
```

```python
import functools
import math

import jax
import jax.numpy as jnp
from jax import lax
from jax.experimental import pallas as pl
from jax.experimental.pallas import tpu as pltpu
from jax.sharding import PartitionSpec as P

VMEM_LIMIT = 48 * 1024 * 1024
UNROLL = 8
UNUSED = 255


class Copies:
    def __init__(self, send_sems):
        self.send_sems = send_sems
        self.started = []

    def send(self, src, dst, recv_sem, device, cond=None):
        copy = pltpu.make_async_remote_copy(
            src_ref=src,
            dst_ref=dst,
            send_sem=self.send_sems.at[len(self.started)],
            recv_sem=recv_sem,
            device_id=device,
            device_id_type=pl.DeviceIdType.MESH,
        )
        self.started.append((cond, copy))
        if cond is None:
            copy.start()
        else:
            pl.when(cond)(lambda: copy.start())

    def wait_recv(self, dst, recv_sem, device):
        pltpu.make_async_remote_copy(
            src_ref=dst,
            dst_ref=dst,
            send_sem=self.send_sems.at[0],
            recv_sem=recv_sem,
            device_id=device,
            device_id_type=pl.DeviceIdType.MESH,
        ).wait_recv()

    def finish(self):
        for cond, copy in self.started:
            if cond is None:
                copy.wait_send()
            else:
                pl.when(cond)(lambda copy=copy: copy.wait_send())


def signal(device):
    pl.semaphore_signal(
        pltpu.get_barrier_semaphore(),
        inc=1,
        device_id=device,
        device_id_type=pl.DeviceIdType.MESH,
    )


def both(x, y):
    return jnp.logical_and(x, y)


def gather_rows_kernel(n_row, own_ref, out_ref, send_sems, recv_sems, local_sem):
    groups = n_row // 2
    half = own_ref.shape[0] // 2
    me = lax.axis_index("row")
    place = me // 2
    core = me % 2
    sibling = {"row": place * 2 + (1 - core)}
    peers = [{"row": lax.rem(place + k, groups) * 2 + core} for k in range(1, groups)]
    for device in [sibling] + peers:
        signal(device)
    keep = pltpu.make_async_copy(own_ref, out_ref.at[me], local_sem)
    keep.start()
    pl.semaphore_wait(pltpu.get_barrier_semaphore(), groups)
    copies = Copies(send_sems)
    for part in range(2):
        rows = pl.ds(part * half, half)
        for device in peers + [sibling]:
            copies.send(
                own_ref.at[rows], out_ref.at[me, rows], recv_sems.at[me, part], device
            )
    for part in range(2):
        rows = pl.ds(part * half, half)
        for k in range(1, groups):
            source = lax.rem(place + groups - k, groups) * 2 + core
            block = out_ref.at[source, rows]
            copies.wait_recv(block, recv_sems.at[source, part], sibling)
            copies.send(block, block, recv_sems.at[source, part], sibling)
    for part in range(2):
        rows = pl.ds(part * half, half)
        for k in range(groups):
            source = lax.rem(place + groups - k, groups) * 2 + (1 - core)
            copies.wait_recv(out_ref.at[source, rows], recv_sems.at[source, part], sibling)
    keep.wait()
    copies.finish()


def gather_rows(features, n_row):
    rows, width = features.shape
    return pl.pallas_call(
        functools.partial(gather_rows_kernel, n_row),
        out_shape=jax.ShapeDtypeStruct((n_row, rows, width), features.dtype),
        in_specs=[pl.BlockSpec(memory_space=pltpu.VMEM)],
        out_specs=pl.BlockSpec(memory_space=pltpu.VMEM),
        scratch_shapes=[
            pltpu.SemaphoreType.DMA((4 * n_row,)),
            pltpu.SemaphoreType.DMA((n_row, 2)),
            pltpu.SemaphoreType.DMA,
        ],
        compiler_params=pltpu.CompilerParams(
            collective_id=0, has_side_effects=True, vmem_limit_bytes=VMEM_LIMIT
        ),
        name="gather_rows",
    )(features)


def spread_kernel(
    forward, rows_ref, cols_ref, count_ref, edges_ref, nodes_ref, out_ref, acc_ref
):
    tile = edges_ref.shape[2]
    edge_count = edges_ref.shape[0]
    acc_ref[...] = jnp.zeros_like(acc_ref)
    column = (
        lax.broadcasted_iota(jnp.int32, (tile // 16, 16, tile), 0) * 16
        + lax.broadcasted_iota(jnp.int32, (tile // 16, 16, tile), 1)
    ).astype(jnp.float32).astype(jnp.bfloat16)
    one = jnp.ones(column.shape, jnp.bfloat16)
    zero = jnp.zeros(column.shape, jnp.bfloat16)

    def pattern(slot):
        total = None
        for k in range(edge_count):
            row = jnp.where(slot < count_ref[0], edges_ref[k, pl.ds(slot, 1), :], UNUSED)
            wide = jnp.broadcast_to(row, (16, tile)).astype(jnp.float32).astype(jnp.bfloat16)
            hit = jnp.where(wide[None] == column, one, zero)
            total = hit if total is None else total + hit
        return total.reshape(tile, tile)

    def body(step, carry):
        first = step * UNROLL
        products = []
        for u in range(UNROLL):
            slot = first + u
            if forward:
                products.append(
                    lax.dot_general(
                        pattern(slot),
                        nodes_ref[cols_ref[slot]],
                        (((0,), (0,)), ((), ())),
                        preferred_element_type=jnp.float32,
                    )
                )
            else:
                products.append(
                    jnp.dot(
                        pattern(slot),
                        nodes_ref[rows_ref[slot]],
                        preferred_element_type=jnp.float32,
                    )
                )
        for u in range(UNROLL):
            slot = first + u
            target = rows_ref[slot] if forward else cols_ref[slot]
            acc_ref[target] += products[u]
        return carry

    steps = lax.div(count_ref[0] + (UNROLL - 1), UNROLL)
    lax.fori_loop(0, steps, body, 0)

    def finish(index, carry):
        out_ref[index] = acc_ref[index].astype(out_ref.dtype)
        return carry

    lax.fori_loop(0, out_ref.shape[0], finish, 0)


def spread(forward, tile_rows, tile_cols, tile_count, edges, nodes, out_tiles):
    tile = edges.shape[2]
    width = nodes.shape[-1]
    node_tiles = nodes.reshape(-1, tile, width)
    smem = pl.BlockSpec(memory_space=pltpu.SMEM)
    vmem = pl.BlockSpec(memory_space=pltpu.VMEM)
    return pl.pallas_call(
        functools.partial(spread_kernel, forward),
        out_shape=jax.ShapeDtypeStruct((out_tiles, tile, width), jnp.bfloat16),
        in_specs=[smem, smem, smem, vmem, vmem],
        out_specs=vmem,
        scratch_shapes=[pltpu.VMEM((out_tiles, tile, width), jnp.float32)],
        compiler_params=pltpu.CompilerParams(vmem_limit_bytes=VMEM_LIMIT),
        cost_estimate=pl.CostEstimate(
            flops=2 * edges.shape[1] * tile * tile * width,
            bytes_accessed=edges.size * 4 + nodes.size * 2 + out_tiles * tile * width * 2,
            transcendentals=0,
        ),
        name="spread_forward" if forward else "spread_back",
    )(tile_rows, tile_cols, tile_count, edges, node_tiles)


def split_rows(rows):
    first_rows = rows * 3 // 16
    return first_rows, (rows - first_rows) // 2


def layer_kernel(
    far,
    near,
    n_row,
    part_ref,
    feat_ref,
    w_self_ref,
    w_neigh_ref,
    cot_ref,
    degree_ref,
    act_ref,
    own_ref,
    share_ref,
    all_ref,
    grad_parts,
    grad_rows,
    below_a,
    above_a,
    below_b,
    above_b,
    cross_a,
    cross_b,
    stage_a,
    stage_b,
    total,
    tmp,
    agg,
    dpre,
    send_sems,
    below_a_sems,
    above_a_sems,
    below_b_sems,
    above_b_sems,
    cross_a_sems,
    cross_b_sems,
    gather_sems,
    grad_sems,
):
    f32, bf16 = jnp.float32, jnp.bfloat16
    rows, width = feat_ref.shape
    first_rows, piece_rows = split_rows(rows)
    first = pl.ds(0, first_rows)
    pieces = [pl.ds(start, piece_rows) for start in range(first_rows, rows, piece_rows)]
    me = lax.axis_index("col")
    a = me // near
    b = me % near

    def at(a_index, b_index):
        return {"col": a_index * near + b_index}

    has_below, has_above = a > 0, a < far - 1
    below, above = at(a - 1, b), at(a + 1, b)
    ahead = [lax.rem(b + k, near) for k in range(1, near)]
    behind = [lax.rem(b + near - k, near) for k in range(1, near)]
    any_peer = at(a, ahead[0]) if near > 1 else at(lax.rem(a + 1, far), b)

    for other in ahead:
        signal(at(a, other))
    pl.when(has_below)(lambda: signal(below))
    pl.when(has_above)(lambda: signal(above))
    row = lax.axis_index("row")
    row_peers = [lax.rem(row + k, n_row) for k in range(1, n_row)]
    for other in row_peers:
        signal({"row": other})
    greeted = n_row - 1 + near - 1 + has_below.astype(jnp.int32) + has_above.astype(jnp.int32)
    pl.semaphore_wait(pltpu.get_barrier_semaphore(), greeted)

    copies = Copies(send_sems)
    up = (1, above, has_below, below_a, below_a_sems, below_b, below_b_sems)
    down = (-1, below, has_above, above_a, above_a_sems, above_b, above_b_sems)

    def reached(index):
        return both(index >= 0, index < far)

    for d in range(far - 1, -1, -1):
        for sign in (1, -1) if d else (1,):
            dest = a + sign * d
            for piece, window in enumerate(pieces):
                for k in range(1, near):
                    copies.send(
                        part_ref.at[dest * near + ahead[k - 1], window],
                        cross_b.at[k - 1, dest, piece],
                        cross_b_sems.at[k - 1, dest, piece],
                        at(a, ahead[k - 1]),
                        reached(dest) if d else None,
                    )
    for d in range(far - 1, 0, -1):
        for sign, onward, arrives, got_a, got_a_sems, got_b, got_b_sems in (up, down):
            dest = a + sign * d
            valid = reached(dest)
            for b_index in range(near):
                j = dest * near + b_index

                @pl.when(both(valid, arrives))
                def _():
                    copies.wait_recv(got_a.at[j], got_a_sems.at[j], any_peer)
                    stage_a[j] = (
                        part_ref[j, first].astype(f32) + got_a[j].astype(f32)
                    ).astype(bf16)

                @pl.when(both(valid, jnp.logical_not(arrives)))
                def _():
                    stage_a[j] = part_ref[j, first]

                copies.send(stage_a.at[j], got_a.at[j], got_a_sems.at[j], onward, valid)
        for piece, window in enumerate(pieces):
            for sign, onward, arrives, got_a, got_a_sems, got_b, got_b_sems in (up, down):
                dest = a + sign * d
                valid = reached(dest)

                @pl.when(valid)
                def _():
                    value = part_ref[dest * near + b, window].astype(f32)
                    for k in range(1, near):
                        copies.wait_recv(
                            cross_b.at[k - 1, dest, piece],
                            cross_b_sems.at[k - 1, dest, piece],
                            any_peer,
                        )
                        value = value + cross_b[k - 1, dest, piece].astype(f32)
                    tmp[...] = value

                @pl.when(both(valid, arrives))
                def _():
                    copies.wait_recv(got_b.at[dest, piece], got_b_sems.at[dest, piece], any_peer)
                    tmp[...] += got_b[dest, piece].astype(f32)

                @pl.when(valid)
                def _():
                    stage_b[dest, piece] = tmp[...].astype(bf16)

                copies.send(
                    stage_b.at[dest, piece],
                    got_b.at[dest, piece],
                    got_b_sems.at[dest, piece],
                    onward,
                    valid,
                )

    def add_both(ref, window, arrived_below, below_sem, arrived_above, above_sem):
        @pl.when(has_below)
        def _():
            copies.wait_recv(arrived_below, below_sem, any_peer)
            ref[window] += arrived_below[...].astype(f32)

        @pl.when(has_above)
        def _():
            copies.wait_recv(arrived_above, above_sem, any_peer)
            ref[window] += arrived_above[...].astype(f32)

    lead = pl.ds(0, first_rows)
    for k in range(1, near):
        j = a * near + ahead[k - 1]
        tmp[lead] = part_ref[j, first].astype(f32)
        add_both(tmp, lead, below_a.at[j], below_a_sems.at[j], above_a.at[j], above_a_sems.at[j])
        stage_a[j] = tmp[lead].astype(bf16)
        copies.send(
            stage_a.at[j], cross_a.at[k - 1], cross_a_sems.at[k - 1], at(a, ahead[k - 1])
        )

    def layer(window):
        degree = degree_ref[window]
        aggregate = (total[window] / degree).astype(bf16)
        agg[window] = aggregate
        preact = jnp.dot(
            feat_ref[window], w_self_ref[...], preferred_element_type=f32
        ) + jnp.dot(aggregate, w_neigh_ref[...], preferred_element_type=f32)
        gate = jax.nn.sigmoid(preact)
        act_ref[window] = (preact * gate).astype(bf16)
        slope = gate * (1.0 + preact * (1.0 - gate))
        dpreact = (cot_ref[window].astype(f32) * slope).astype(bf16)
        dpre[window] = dpreact
        back = lax.dot_general(
            dpreact, w_neigh_ref[...], (((1,), (1,)), ((), ())), preferred_element_type=f32
        )
        all_ref[me, window] = (back / degree).astype(bf16)

    def hand_on(j, window, part, device, cond=None):
        copies.send(
            all_ref.at[j, window], all_ref.at[j, window], gather_sems.at[part, j], device, cond
        )

    def arrive(j, window, part):
        copies.wait_recv(all_ref.at[j, window], gather_sems.at[part, j], any_peer)

    for piece, window in enumerate(pieces):
        total[window] = part_ref[me, window].astype(f32)
        for k in range(1, near):
            copies.wait_recv(
                cross_b.at[k - 1, a, piece], cross_b_sems.at[k - 1, a, piece], any_peer
            )
            total[window] += cross_b[k - 1, a, piece].astype(f32)
        add_both(
            total,
            window,
            below_b.at[a, piece],
            below_b_sems.at[a, piece],
            above_b.at[a, piece],
            above_b_sems.at[a, piece],
        )
        layer(window)
        hand_on(me, window, piece, above, has_above)
        hand_on(me, window, piece, below, has_below)
        for other in ahead:
            hand_on(me, window, piece, at(a, other))
    total[first] = part_ref[me, first].astype(f32)
    add_both(
        total, first, below_a.at[me], below_a_sems.at[me], above_a.at[me], above_a_sems.at[me]
    )
    for k in range(1, near):
        copies.wait_recv(cross_a.at[k - 1], cross_a_sems.at[k - 1], any_peer)
        total[first] += cross_a[k - 1].astype(f32)
    layer(first)
    last = len(pieces)
    for other in ahead:
        hand_on(me, first, last, at(a, other))
    hand_on(me, first, last, above, has_above)
    hand_on(me, first, last, below, has_below)

    contract_rows = (((0,), (0,)), ((), ()))

    def own_grad():
        own_ref[...] = lax.dot_general(
            dpre[...], w_self_ref[...], (((1,), (1,)), ((), ())), preferred_element_type=f32
        )

    chunk = grad_parts.shape[1]

    def weight_grad(matrix, left_ref):
        product = lax.dot_general(
            left_ref[...], dpre[...], contract_rows, preferred_element_type=f32
        ).astype(bf16)
        shares = n_row // 2
        for t in range(shares):
            grad_parts[matrix * shares + t] = product[t * chunk : (t + 1) * chunk]

    def grad_self():
        weight_grad(0, feat_ref)

    def grad_neigh():
        weight_grad(1, agg)
        for k, other in enumerate(row_peers):
            copies.send(grad_parts.at[other], grad_rows.at[k], grad_sems.at[k], {"row": other})

    beside = [own_grad, grad_self, grad_neigh]
    beside.pop(0)()
    sides = ((1, above, has_above), (-1, below, has_below))
    for d in range(far):
        if d:
            for piece, window in enumerate(pieces):
                for sign, onward, goes_on in sides:
                    source = a - sign * d
                    valid = reached(source)
                    j = source * near + b
                    pl.when(valid)(lambda: arrive(j, window, piece))
                    hand_on(j, window, piece, onward, both(valid, goes_on))
                    for other in ahead:
                        hand_on(j, window, piece, at(a, other), valid)
            for sign, onward, goes_on in sides:
                source = a - sign * d
                valid = reached(source)
                for b_index in range(near):
                    j = source * near + b_index
                    pl.when(valid)(lambda: arrive(j, first, last))
                    hand_on(j, first, last, onward, both(valid, goes_on))
        else:
            for other in behind:
                j = a * near + other
                arrive(j, first, last)
                hand_on(j, first, last, above, has_above)
                hand_on(j, first, last, below, has_below)
        if beside:
            beside.pop(0)()
    for step in beside:
        step()
    for a_index in range(far):
        for other in behind:
            for piece, window in enumerate(pieces):
                arrive(a_index * near + other, window, piece)
    share = grad_parts[row].astype(f32)
    for k in range(n_row - 1):
        copies.wait_recv(grad_rows.at[k], grad_sems.at[k], any_peer)
        share = share + grad_rows[k].astype(f32)
    share_ref[...] = share
    copies.finish()


def layer_call(partials, features, w_self, w_neigh, cotangent, degree, n_row, n_col):
    far = 4 if n_col % 4 == 0 else n_col
    near = n_col // far
    rows, width = features.shape
    first_rows, piece_rows = split_rows(rows)
    bf16, f32 = jnp.bfloat16, jnp.float32
    vmem = pl.BlockSpec(memory_space=pltpu.VMEM)
    crosses = max(near - 1, 1)
    dma = pltpu.SemaphoreType.DMA
    return pl.pallas_call(
        functools.partial(layer_kernel, far, near, n_row),
        out_shape=(
            jax.ShapeDtypeStruct((rows, width), bf16),
            jax.ShapeDtypeStruct((rows, width), f32),
            jax.ShapeDtypeStruct((2 * width // n_row, width), f32),
            jax.ShapeDtypeStruct((n_col, rows, width), bf16),
        ),
        in_specs=[vmem] * 6,
        out_specs=(vmem,) * 4,
        scratch_shapes=[
            pltpu.VMEM((n_row, 2 * width // n_row, width), bf16),
            pltpu.VMEM((n_row - 1, 2 * width // n_row, width), bf16),
            pltpu.VMEM((n_col, first_rows, width), bf16),
            pltpu.VMEM((n_col, first_rows, width), bf16),
            pltpu.VMEM((far, 2, piece_rows, width), bf16),
            pltpu.VMEM((far, 2, piece_rows, width), bf16),
            pltpu.VMEM((crosses, first_rows, width), bf16),
            pltpu.VMEM((crosses, far, 2, piece_rows, width), bf16),
            pltpu.VMEM((n_col, first_rows, width), bf16),
            pltpu.VMEM((far, 2, piece_rows, width), bf16),
            pltpu.VMEM((rows, width), f32),
            pltpu.VMEM((piece_rows, width), f32),
            pltpu.VMEM((rows, width), bf16),
            pltpu.VMEM((rows, width), bf16),
            dma((24 * n_col + n_row,)),
            dma((n_col,)),
            dma((n_col,)),
            dma((far, 2)),
            dma((far, 2)),
            dma((crosses,)),
            dma((crosses, far, 2)),
            dma((3, n_col)),
            dma((n_row - 1,)),
        ],
        compiler_params=pltpu.CompilerParams(
            collective_id=1, has_side_effects=True, vmem_limit_bytes=VMEM_LIMIT
        ),
        name="layer",
    )(partials, features, w_self, w_neigh, cotangent, degree)


def scatter_rows_kernel(
    n_row,
    n_col,
    scale,
    part_ref,
    own_ref,
    share_ref,
    out_ref,
    grad_self_ref,
    grad_neigh_ref,
    from_sibling,
    staged,
    from_peer,
    total,
    grad_cols,
    grad_all,
    send_sems,
    sibling_sems,
    peer_sems,
    grad_col_sems,
    grad_piece_sems,
    grad_all_sems,
):
    f32 = jnp.float32
    chunk = share_ref.shape[0]
    piece = grad_cols.shape[1]
    owners = chunk // piece
    column = lax.axis_index("col")
    far_cols = [lax.rem(column + k, n_col) for k in range(1, n_col)]
    groups = n_row // 2
    half = own_ref.shape[0] // 2
    width = own_ref.shape[1]
    me = lax.axis_index("row")
    place = me // 2
    core = me % 2
    sibling = {"row": place * 2 + (1 - core)}
    peers = [lax.rem(place + k, groups) for k in range(1, groups)]
    all_rows = [lax.rem(me + k, n_row) for k in range(1, n_row)]
    for other in all_rows:
        signal({"row": other})
    for other in far_cols:
        signal({"col": other})
    pl.semaphore_wait(pltpu.get_barrier_semaphore(), n_row - 1 + n_col - 1)
    copies = Copies(send_sems)
    owns = column < owners
    mine = pl.ds(pl.multiple_of(column * piece, piece), piece)
    for j in range(owners):
        slot = jnp.maximum(lax.rem(j - column + n_col, n_col) - 1, 0)
        copies.send(
            share_ref.at[pl.ds(j * piece, piece)],
            grad_cols.at[slot],
            grad_col_sems.at[slot],
            {"col": j},
            column != j,
        )
    windows = [pl.ds(part * half, half) for part in range(2)]
    for peer in peers + [place]:
        for part, rows in enumerate(windows):
            copies.send(
                part_ref.at[peer * 2 + (1 - core), rows],
                from_sibling.at[peer, rows],
                sibling_sems.at[peer, part],
                sibling,
            )
    for k, peer in enumerate(peers):
        for part, rows in enumerate(windows):
            copies.wait_recv(from_sibling.at[peer, rows], sibling_sems.at[peer, part], sibling)
            staged[k, rows] = (
                part_ref[peer * 2 + core, rows].astype(f32)
                + from_sibling[peer, rows].astype(f32)
            ).astype(staged.dtype)
            copies.send(
                staged.at[k, rows],
                from_peer.at[k, rows],
                peer_sems.at[k, part],
                {"row": peer * 2 + core},
            )

    @pl.when(owns)
    def _():
        share = share_ref[mine]
        for k in range(n_col - 1):
            copies.wait_recv(grad_cols.at[k], grad_col_sems.at[k], sibling)
            share = share + grad_cols[k]
        grad_all[me, mine] = (share * scale).astype(grad_all.dtype)

    for other in far_cols:
        copies.send(
            grad_all.at[me, mine],
            grad_all.at[me, mine],
            grad_piece_sems.at[jnp.minimum(column, owners - 1)],
            {"col": other},
            owns,
        )
    for part, rows in enumerate(windows):
        copies.wait_recv(from_sibling.at[place, rows], sibling_sems.at[place, part], sibling)
        total[rows] = (
            own_ref[rows]
            + part_ref[me, rows].astype(f32)
            + from_sibling[place, rows].astype(f32)
        )
    for j in range(owners):
        block = grad_all.at[me, pl.ds(j * piece, piece)]
        pl.when(column != j)(
            lambda: copies.wait_recv(block, grad_piece_sems.at[j], sibling)
        )
    for other in all_rows:
        copies.send(grad_all.at[me], grad_all.at[me], grad_all_sems.at[me], {"row": other})
    for part, rows in enumerate(windows):
        value = total[rows]
        for k in range(groups - 1):
            copies.wait_recv(from_peer.at[k, rows], peer_sems.at[k, part], sibling)
            value = value + from_peer[k, rows].astype(f32)
        out_ref[rows] = value.astype(out_ref.dtype)
    for other in all_rows:
        copies.wait_recv(grad_all.at[other], grad_all_sems.at[other], sibling)
    shares = n_row // 2
    for j in range(n_row):
        ref = (grad_self_ref, grad_neigh_ref)[j // shares]
        ref[pl.ds(j % shares * chunk, chunk)] = grad_all[j].astype(f32)
    copies.finish()


def scatter_rows(partials, own_grad, share, n_row, n_col, scale):
    rows, width = own_grad.shape
    groups = n_row // 2
    others = max(groups - 1, 1)
    chunk = share.shape[0]
    piece = max(chunk // n_col, 16)
    owners = chunk // piece
    vmem = pl.BlockSpec(memory_space=pltpu.VMEM)
    bf16 = jnp.bfloat16
    dma = pltpu.SemaphoreType.DMA
    return pl.pallas_call(
        functools.partial(scatter_rows_kernel, n_row, n_col, scale),
        out_shape=(
            jax.ShapeDtypeStruct((rows, width), bf16),
            jax.ShapeDtypeStruct((width, width), jnp.float32),
            jax.ShapeDtypeStruct((width, width), jnp.float32),
        ),
        in_specs=[vmem] * 3,
        out_specs=(vmem,) * 3,
        scratch_shapes=[
            pltpu.VMEM((groups, rows, width), bf16),
            pltpu.VMEM((others, rows, width), bf16),
            pltpu.VMEM((others, rows, width), bf16),
            pltpu.VMEM((rows, width), jnp.float32),
            pltpu.VMEM((n_col - 1, piece, width), jnp.float32),
            pltpu.VMEM((n_row, chunk, width), bf16),
            dma((4 * groups + 2 * n_col + n_row,)),
            dma((groups, 2)),
            dma((others, 2)),
            dma((n_col - 1,)),
            dma((owners,)),
            dma((n_row,)),
        ],
        compiler_params=pltpu.CompilerParams(
            collective_id=2, has_side_effects=True, vmem_limit_bytes=VMEM_LIMIT
        ),
        name="scatter_rows",
    )(partials, own_grad, share)


def per_device(
    features, w_self, w_neigh, cotangent, degree, tile_rows, tile_cols, tile_edges, tile_count
):
    rows, width = features.shape
    tile = tile_edges.shape[2]
    slots = tile_rows.shape[0]
    n_row = lax.axis_size("row")
    n_col = lax.axis_size("col")
    edges = tile_edges
    padding = (-slots) % UNROLL
    if padding:
        edges = jnp.pad(edges, ((0, 0), (0, padding), (0, 0)))
        tile_rows = jnp.pad(tile_rows, (0, padding))
        tile_cols = jnp.pad(tile_cols, (0, padding))
    degree_wide = degree.astype(jnp.float32)[:, None]

    column_nodes = gather_rows(features, n_row)
    partial_sums = spread(
        True, tile_rows, tile_cols, tile_count, edges, column_nodes, rows * n_col // tile
    )
    activations, own_grad, share, row_nodes = layer_call(
        partial_sums.reshape(n_col, rows, width),
        features,
        w_self,
        w_neigh,
        cotangent,
        degree_wide,
        n_row,
        n_col,
    )
    partial_grads = spread(
        False, tile_rows, tile_cols, tile_count, edges, row_nodes, rows * n_row // tile
    )
    scale = 1.0 / math.sqrt(rows * n_row * n_col)
    feature_grad, grad_self, grad_neigh = scatter_rows(
        partial_grads.reshape(n_row, rows, width), own_grad, share, n_row, n_col, scale
    )
    return (activations, feature_grad, grad_self, grad_neigh)


def solution(mesh):
    nodes = P(("row", "col"), None)
    flat = P(("row", "col"))
    return jax.shard_map(
        per_device,
        mesh=mesh,
        in_specs=(nodes, P(), P(), nodes, flat, flat, flat, P(None, ("row", "col"), None), flat),
        out_specs=(nodes, nodes, P(), P()),
        check_vma=False,
    )
```

```python
import functools
import math

import jax
import jax.numpy as jnp
from jax import lax
from jax.experimental import pallas as pl
from jax.experimental.pallas import tpu as pltpu
from jax.sharding import PartitionSpec as P

VMEM_LIMIT = 48 * 1024 * 1024
UNROLL = 16
UNUSED = 255


class Copies:
    def __init__(self, send_sems):
        self.send_sems = send_sems
        self.started = []

    def send(self, src, dst, recv_sem, device, cond=None):
        copy = pltpu.make_async_remote_copy(
            src_ref=src,
            dst_ref=dst,
            send_sem=self.send_sems.at[len(self.started)],
            recv_sem=recv_sem,
            device_id=device,
            device_id_type=pl.DeviceIdType.MESH,
        )
        self.started.append((cond, copy))
        if cond is None:
            copy.start()
        else:
            pl.when(cond)(lambda: copy.start())

    def wait_recv(self, dst, recv_sem, device):
        pltpu.make_async_remote_copy(
            src_ref=dst,
            dst_ref=dst,
            send_sem=self.send_sems.at[0],
            recv_sem=recv_sem,
            device_id=device,
            device_id_type=pl.DeviceIdType.MESH,
        ).wait_recv()

    def finish(self):
        for cond, copy in self.started:
            if cond is None:
                copy.wait_send()
            else:
                pl.when(cond)(lambda copy=copy: copy.wait_send())


def signal(device):
    pl.semaphore_signal(
        pltpu.get_barrier_semaphore(),
        inc=1,
        device_id=device,
        device_id_type=pl.DeviceIdType.MESH,
    )


def both(x, y):
    return jnp.logical_and(x, y)


def gather_rows_kernel(n_row, own_ref, out_ref, send_sems, recv_sems, local_sem):
    groups = n_row // 2
    half = own_ref.shape[0] // 2
    me = lax.axis_index("row")
    place = me // 2
    core = me % 2
    sibling = {"row": place * 2 + (1 - core)}
    peers = [{"row": lax.rem(place + k, groups) * 2 + core} for k in range(1, groups)]
    for device in [sibling] + peers:
        signal(device)
    keep = pltpu.make_async_copy(own_ref, out_ref.at[me], local_sem)
    keep.start()
    pl.semaphore_wait(pltpu.get_barrier_semaphore(), groups)
    copies = Copies(send_sems)
    for part in range(2):
        rows = pl.ds(part * half, half)
        for device in peers + [sibling]:
            copies.send(
                own_ref.at[rows], out_ref.at[me, rows], recv_sems.at[me, part], device
            )
    for part in range(2):
        rows = pl.ds(part * half, half)
        for k in range(1, groups):
            source = lax.rem(place + groups - k, groups) * 2 + core
            block = out_ref.at[source, rows]
            copies.wait_recv(block, recv_sems.at[source, part], sibling)
            copies.send(block, block, recv_sems.at[source, part], sibling)
    for part in range(2):
        rows = pl.ds(part * half, half)
        for k in range(groups):
            source = lax.rem(place + groups - k, groups) * 2 + (1 - core)
            copies.wait_recv(out_ref.at[source, rows], recv_sems.at[source, part], sibling)
    keep.wait()
    copies.finish()


def gather_rows(features, n_row):
    rows, width = features.shape
    return pl.pallas_call(
        functools.partial(gather_rows_kernel, n_row),
        out_shape=jax.ShapeDtypeStruct((n_row, rows, width), features.dtype),
        in_specs=[pl.BlockSpec(memory_space=pltpu.VMEM)],
        out_specs=pl.BlockSpec(memory_space=pltpu.VMEM),
        scratch_shapes=[
            pltpu.SemaphoreType.DMA((4 * n_row,)),
            pltpu.SemaphoreType.DMA((n_row, 2)),
            pltpu.SemaphoreType.DMA,
        ],
        compiler_params=pltpu.CompilerParams(
            collective_id=0, has_side_effects=True, vmem_limit_bytes=VMEM_LIMIT
        ),
        name="gather_rows",
    )(features)


def spread_kernel(
    forward, rows_ref, cols_ref, count_ref, edges_ref, nodes_ref, out_ref, acc_ref
):
    tile = edges_ref.shape[2]
    edge_count = edges_ref.shape[0]
    acc_ref[...] = jnp.zeros_like(acc_ref)
    column = (
        lax.broadcasted_iota(jnp.int32, (tile // 16, 16, tile), 0) * 16
        + lax.broadcasted_iota(jnp.int32, (tile // 16, 16, tile), 1)
    ).astype(jnp.float32).astype(jnp.bfloat16)
    one = jnp.ones(column.shape, jnp.bfloat16)
    zero = jnp.zeros(column.shape, jnp.bfloat16)

    def pattern(slot):
        total = None
        for k in range(edge_count):
            row = jnp.where(slot < count_ref[0], edges_ref[k, pl.ds(slot, 1), :], UNUSED)
            wide = jnp.broadcast_to(row, (16, tile)).astype(jnp.float32).astype(jnp.bfloat16)
            hit = jnp.where(wide[None] == column, one, zero)
            total = hit if total is None else total + hit
        return total.reshape(tile, tile)

    def body(step, carry):
        first = step * UNROLL
        products = []
        for u in range(UNROLL):
            slot = first + u
            if forward:
                products.append(
                    lax.dot_general(
                        pattern(slot),
                        nodes_ref[cols_ref[slot]],
                        (((0,), (0,)), ((), ())),
                        preferred_element_type=jnp.float32,
                    )
                )
            else:
                products.append(
                    jnp.dot(
                        pattern(slot),
                        nodes_ref[rows_ref[slot]],
                        preferred_element_type=jnp.float32,
                    )
                )
        for u in range(UNROLL):
            slot = first + u
            target = rows_ref[slot] if forward else cols_ref[slot]
            acc_ref[target] += products[u]
        return carry

    steps = lax.div(count_ref[0] + (UNROLL - 1), UNROLL)
    lax.fori_loop(0, steps, body, 0)

    def finish(index, carry):
        out_ref[index] = acc_ref[index].astype(out_ref.dtype)
        return carry

    lax.fori_loop(0, out_ref.shape[0], finish, 0)


def spread(forward, tile_rows, tile_cols, tile_count, edges, nodes, out_tiles):
    tile = edges.shape[2]
    width = nodes.shape[-1]
    node_tiles = nodes.reshape(-1, tile, width)
    smem = pl.BlockSpec(memory_space=pltpu.SMEM)
    vmem = pl.BlockSpec(memory_space=pltpu.VMEM)
    return pl.pallas_call(
        functools.partial(spread_kernel, forward),
        out_shape=jax.ShapeDtypeStruct((out_tiles, tile, width), jnp.bfloat16),
        in_specs=[smem, smem, smem, vmem, vmem],
        out_specs=vmem,
        scratch_shapes=[pltpu.VMEM((out_tiles, tile, width), jnp.float32)],
        compiler_params=pltpu.CompilerParams(vmem_limit_bytes=VMEM_LIMIT),
        cost_estimate=pl.CostEstimate(
            flops=2 * edges.shape[1] * tile * tile * width,
            bytes_accessed=edges.size * 4 + nodes.size * 2 + out_tiles * tile * width * 2,
            transcendentals=0,
        ),
        name="spread_forward" if forward else "spread_back",
    )(tile_rows, tile_cols, tile_count, edges, node_tiles)


def split_rows(rows):
    first_rows = rows * 3 // 16
    return first_rows, (rows - first_rows) // 2


def layer_kernel(
    far,
    near,
    n_row,
    part_ref,
    feat_ref,
    w_self_ref,
    w_neigh_ref,
    cot_ref,
    degree_ref,
    act_ref,
    own_ref,
    share_ref,
    all_ref,
    grad_parts,
    grad_rows,
    below_a,
    above_a,
    below_b,
    above_b,
    cross_a,
    cross_b,
    stage_a,
    stage_b,
    total,
    tmp,
    agg,
    dpre,
    send_sems,
    below_a_sems,
    above_a_sems,
    below_b_sems,
    above_b_sems,
    cross_a_sems,
    cross_b_sems,
    gather_sems,
    grad_sems,
):
    f32, bf16 = jnp.float32, jnp.bfloat16
    rows, width = feat_ref.shape
    first_rows, piece_rows = split_rows(rows)
    first = pl.ds(0, first_rows)
    pieces = [pl.ds(start, piece_rows) for start in range(first_rows, rows, piece_rows)]
    me = lax.axis_index("col")
    a = me // near
    b = me % near

    def at(a_index, b_index):
        return {"col": a_index * near + b_index}

    has_below, has_above = a > 0, a < far - 1
    below, above = at(a - 1, b), at(a + 1, b)
    ahead = [lax.rem(b + k, near) for k in range(1, near)]
    behind = [lax.rem(b + near - k, near) for k in range(1, near)]
    any_peer = at(a, ahead[0]) if near > 1 else at(lax.rem(a + 1, far), b)

    for other in ahead:
        signal(at(a, other))
    pl.when(has_below)(lambda: signal(below))
    pl.when(has_above)(lambda: signal(above))
    row = lax.axis_index("row")
    row_peers = [lax.rem(row + k, n_row) for k in range(1, n_row)]
    for other in row_peers:
        signal({"row": other})
    greeted = n_row - 1 + near - 1 + has_below.astype(jnp.int32) + has_above.astype(jnp.int32)
    pl.semaphore_wait(pltpu.get_barrier_semaphore(), greeted)

    copies = Copies(send_sems)
    up = (1, above, has_below, below_a, below_a_sems, below_b, below_b_sems)
    down = (-1, below, has_above, above_a, above_a_sems, above_b, above_b_sems)

    def reached(index):
        return both(index >= 0, index < far)

    for d in range(far - 1, -1, -1):
        for sign in (1, -1) if d else (1,):
            dest = a + sign * d
            for piece, window in enumerate(pieces):
                for k in range(1, near):
                    copies.send(
                        part_ref.at[dest * near + ahead[k - 1], window],
                        cross_b.at[k - 1, dest, piece],
                        cross_b_sems.at[k - 1, dest, piece],
                        at(a, ahead[k - 1]),
                        reached(dest) if d else None,
                    )
    for d in range(far - 1, 0, -1):
        for sign, onward, arrives, got_a, got_a_sems, got_b, got_b_sems in (up, down):
            dest = a + sign * d
            valid = reached(dest)
            for b_index in range(near):
                j = dest * near + b_index

                @pl.when(both(valid, arrives))
                def _():
                    copies.wait_recv(got_a.at[j], got_a_sems.at[j], any_peer)
                    stage_a[j] = (
                        part_ref[j, first].astype(f32) + got_a[j].astype(f32)
                    ).astype(bf16)

                @pl.when(both(valid, jnp.logical_not(arrives)))
                def _():
                    stage_a[j] = part_ref[j, first]

                copies.send(stage_a.at[j], got_a.at[j], got_a_sems.at[j], onward, valid)
        for piece, window in enumerate(pieces):
            for sign, onward, arrives, got_a, got_a_sems, got_b, got_b_sems in (up, down):
                dest = a + sign * d
                valid = reached(dest)

                @pl.when(valid)
                def _():
                    value = part_ref[dest * near + b, window].astype(f32)
                    for k in range(1, near):
                        copies.wait_recv(
                            cross_b.at[k - 1, dest, piece],
                            cross_b_sems.at[k - 1, dest, piece],
                            any_peer,
                        )
                        value = value + cross_b[k - 1, dest, piece].astype(f32)
                    tmp[...] = value

                @pl.when(both(valid, arrives))
                def _():
                    copies.wait_recv(got_b.at[dest, piece], got_b_sems.at[dest, piece], any_peer)
                    tmp[...] += got_b[dest, piece].astype(f32)

                @pl.when(valid)
                def _():
                    stage_b[dest, piece] = tmp[...].astype(bf16)

                copies.send(
                    stage_b.at[dest, piece],
                    got_b.at[dest, piece],
                    got_b_sems.at[dest, piece],
                    onward,
                    valid,
                )

    def add_both(ref, window, arrived_below, below_sem, arrived_above, above_sem):
        @pl.when(has_below)
        def _():
            copies.wait_recv(arrived_below, below_sem, any_peer)
            ref[window] += arrived_below[...].astype(f32)

        @pl.when(has_above)
        def _():
            copies.wait_recv(arrived_above, above_sem, any_peer)
            ref[window] += arrived_above[...].astype(f32)

    lead = pl.ds(0, first_rows)
    for k in range(1, near):
        j = a * near + ahead[k - 1]
        tmp[lead] = part_ref[j, first].astype(f32)
        add_both(tmp, lead, below_a.at[j], below_a_sems.at[j], above_a.at[j], above_a_sems.at[j])
        stage_a[j] = tmp[lead].astype(bf16)
        copies.send(
            stage_a.at[j], cross_a.at[k - 1], cross_a_sems.at[k - 1], at(a, ahead[k - 1])
        )

    def layer(window):
        degree = degree_ref[window]
        aggregate = (total[window] / degree).astype(bf16)
        agg[window] = aggregate
        preact = jnp.dot(
            feat_ref[window], w_self_ref[...], preferred_element_type=f32
        ) + jnp.dot(aggregate, w_neigh_ref[...], preferred_element_type=f32)
        gate = jax.nn.sigmoid(preact)
        act_ref[window] = (preact * gate).astype(bf16)
        slope = gate * (1.0 + preact * (1.0 - gate))
        dpreact = (cot_ref[window].astype(f32) * slope).astype(bf16)
        dpre[window] = dpreact
        back = lax.dot_general(
            dpreact, w_neigh_ref[...], (((1,), (1,)), ((), ())), preferred_element_type=f32
        )
        all_ref[me, window] = (back / degree).astype(bf16)

    def hand_on(j, window, part, device, cond=None):
        copies.send(
            all_ref.at[j, window], all_ref.at[j, window], gather_sems.at[part, j], device, cond
        )

    def arrive(j, window, part):
        copies.wait_recv(all_ref.at[j, window], gather_sems.at[part, j], any_peer)

    for piece, window in enumerate(pieces):
        total[window] = part_ref[me, window].astype(f32)
        for k in range(1, near):
            copies.wait_recv(
                cross_b.at[k - 1, a, piece], cross_b_sems.at[k - 1, a, piece], any_peer
            )
            total[window] += cross_b[k - 1, a, piece].astype(f32)
        add_both(
            total,
            window,
            below_b.at[a, piece],
            below_b_sems.at[a, piece],
            above_b.at[a, piece],
            above_b_sems.at[a, piece],
        )
        layer(window)
        hand_on(me, window, piece, above, has_above)
        hand_on(me, window, piece, below, has_below)
        for other in ahead:
            hand_on(me, window, piece, at(a, other))
    total[first] = part_ref[me, first].astype(f32)
    add_both(
        total, first, below_a.at[me], below_a_sems.at[me], above_a.at[me], above_a_sems.at[me]
    )
    for k in range(1, near):
        copies.wait_recv(cross_a.at[k - 1], cross_a_sems.at[k - 1], any_peer)
        total[first] += cross_a[k - 1].astype(f32)
    layer(first)
    last = len(pieces)
    for other in ahead:
        hand_on(me, first, last, at(a, other))
    hand_on(me, first, last, above, has_above)
    hand_on(me, first, last, below, has_below)

    contract_rows = (((0,), (0,)), ((), ()))

    def own_grad():
        own_ref[...] = lax.dot_general(
            dpre[...], w_self_ref[...], (((1,), (1,)), ((), ())), preferred_element_type=f32
        )

    chunk = grad_parts.shape[1]

    def weight_grad(matrix, left_ref):
        product = lax.dot_general(
            left_ref[...], dpre[...], contract_rows, preferred_element_type=f32
        ).astype(bf16)
        shares = n_row // 2
        for t in range(shares):
            grad_parts[matrix * shares + t] = product[t * chunk : (t + 1) * chunk]

    def grad_self():
        weight_grad(0, feat_ref)

    def grad_neigh():
        weight_grad(1, agg)
        for k, other in enumerate(row_peers):
            copies.send(grad_parts.at[other], grad_rows.at[k], grad_sems.at[k], {"row": other})

    beside = [own_grad, grad_self, grad_neigh]
    beside.pop(0)()
    sides = ((1, above, has_above), (-1, below, has_below))
    for d in range(far):
        if d:
            for piece, window in enumerate(pieces):
                for sign, onward, goes_on in sides:
                    source = a - sign * d
                    valid = reached(source)
                    j = source * near + b
                    pl.when(valid)(lambda: arrive(j, window, piece))
                    hand_on(j, window, piece, onward, both(valid, goes_on))
                    for other in ahead:
                        hand_on(j, window, piece, at(a, other), valid)
            for sign, onward, goes_on in sides:
                source = a - sign * d
                valid = reached(source)
                for b_index in range(near):
                    j = source * near + b_index
                    pl.when(valid)(lambda: arrive(j, first, last))
                    hand_on(j, first, last, onward, both(valid, goes_on))
        else:
            for other in behind:
                j = a * near + other
                arrive(j, first, last)
                hand_on(j, first, last, above, has_above)
                hand_on(j, first, last, below, has_below)
        if beside:
            beside.pop(0)()
    for step in beside:
        step()
    for a_index in range(far):
        for other in behind:
            for piece, window in enumerate(pieces):
                arrive(a_index * near + other, window, piece)
    share = grad_parts[row].astype(f32)
    for k in range(n_row - 1):
        copies.wait_recv(grad_rows.at[k], grad_sems.at[k], any_peer)
        share = share + grad_rows[k].astype(f32)
    share_ref[...] = share
    copies.finish()


def layer_call(partials, features, w_self, w_neigh, cotangent, degree, n_row, n_col):
    far = 4 if n_col % 4 == 0 else n_col
    near = n_col // far
    rows, width = features.shape
    first_rows, piece_rows = split_rows(rows)
    bf16, f32 = jnp.bfloat16, jnp.float32
    vmem = pl.BlockSpec(memory_space=pltpu.VMEM)
    crosses = max(near - 1, 1)
    dma = pltpu.SemaphoreType.DMA
    return pl.pallas_call(
        functools.partial(layer_kernel, far, near, n_row),
        out_shape=(
            jax.ShapeDtypeStruct((rows, width), bf16),
            jax.ShapeDtypeStruct((rows, width), f32),
            jax.ShapeDtypeStruct((2 * width // n_row, width), f32),
            jax.ShapeDtypeStruct((n_col, rows, width), bf16),
        ),
        in_specs=[vmem] * 6,
        out_specs=(vmem,) * 4,
        scratch_shapes=[
            pltpu.VMEM((n_row, 2 * width // n_row, width), bf16),
            pltpu.VMEM((n_row - 1, 2 * width // n_row, width), bf16),
            pltpu.VMEM((n_col, first_rows, width), bf16),
            pltpu.VMEM((n_col, first_rows, width), bf16),
            pltpu.VMEM((far, 2, piece_rows, width), bf16),
            pltpu.VMEM((far, 2, piece_rows, width), bf16),
            pltpu.VMEM((crosses, first_rows, width), bf16),
            pltpu.VMEM((crosses, far, 2, piece_rows, width), bf16),
            pltpu.VMEM((n_col, first_rows, width), bf16),
            pltpu.VMEM((far, 2, piece_rows, width), bf16),
            pltpu.VMEM((rows, width), f32),
            pltpu.VMEM((piece_rows, width), f32),
            pltpu.VMEM((rows, width), bf16),
            pltpu.VMEM((rows, width), bf16),
            dma((24 * n_col + n_row,)),
            dma((n_col,)),
            dma((n_col,)),
            dma((far, 2)),
            dma((far, 2)),
            dma((crosses,)),
            dma((crosses, far, 2)),
            dma((3, n_col)),
            dma((n_row - 1,)),
        ],
        compiler_params=pltpu.CompilerParams(
            collective_id=1, has_side_effects=True, vmem_limit_bytes=VMEM_LIMIT
        ),
        name="layer",
    )(partials, features, w_self, w_neigh, cotangent, degree)


def scatter_rows_kernel(
    n_row,
    n_col,
    scale,
    part_ref,
    own_ref,
    share_ref,
    out_ref,
    grad_self_ref,
    grad_neigh_ref,
    from_sibling,
    staged,
    from_peer,
    total,
    grad_cols,
    grad_all,
    send_sems,
    sibling_sems,
    peer_sems,
    grad_col_sems,
    grad_piece_sems,
    grad_all_sems,
):
    f32 = jnp.float32
    chunk = share_ref.shape[0]
    piece = grad_cols.shape[1]
    owners = chunk // piece
    column = lax.axis_index("col")
    far_cols = [lax.rem(column + k, n_col) for k in range(1, n_col)]
    groups = n_row // 2
    half = own_ref.shape[0] // 2
    width = own_ref.shape[1]
    me = lax.axis_index("row")
    place = me // 2
    core = me % 2
    sibling = {"row": place * 2 + (1 - core)}
    peers = [lax.rem(place + k, groups) for k in range(1, groups)]
    all_rows = [lax.rem(me + k, n_row) for k in range(1, n_row)]
    for other in all_rows:
        signal({"row": other})
    for other in far_cols:
        signal({"col": other})
    pl.semaphore_wait(pltpu.get_barrier_semaphore(), n_row - 1 + n_col - 1)
    copies = Copies(send_sems)
    owns = column < owners
    mine = pl.ds(pl.multiple_of(column * piece, piece), piece)
    for j in range(owners):
        slot = jnp.maximum(lax.rem(j - column + n_col, n_col) - 1, 0)
        copies.send(
            share_ref.at[pl.ds(j * piece, piece)],
            grad_cols.at[slot],
            grad_col_sems.at[slot],
            {"col": j},
            column != j,
        )
    windows = [pl.ds(part * half, half) for part in range(2)]
    for peer in peers + [place]:
        for part, rows in enumerate(windows):
            copies.send(
                part_ref.at[peer * 2 + (1 - core), rows],
                from_sibling.at[peer, rows],
                sibling_sems.at[peer, part],
                sibling,
            )
    for k, peer in enumerate(peers):
        for part, rows in enumerate(windows):
            copies.wait_recv(from_sibling.at[peer, rows], sibling_sems.at[peer, part], sibling)
            staged[k, rows] = (
                part_ref[peer * 2 + core, rows].astype(f32)
                + from_sibling[peer, rows].astype(f32)
            ).astype(staged.dtype)
            copies.send(
                staged.at[k, rows],
                from_peer.at[k, rows],
                peer_sems.at[k, part],
                {"row": peer * 2 + core},
            )

    @pl.when(owns)
    def _():
        share = share_ref[mine]
        for k in range(n_col - 1):
            copies.wait_recv(grad_cols.at[k], grad_col_sems.at[k], sibling)
            share = share + grad_cols[k]
        grad_all[me, mine] = (share * scale).astype(grad_all.dtype)

    for other in far_cols:
        copies.send(
            grad_all.at[me, mine],
            grad_all.at[me, mine],
            grad_piece_sems.at[jnp.minimum(column, owners - 1)],
            {"col": other},
            owns,
        )
    for part, rows in enumerate(windows):
        copies.wait_recv(from_sibling.at[place, rows], sibling_sems.at[place, part], sibling)
        total[rows] = (
            own_ref[rows]
            + part_ref[me, rows].astype(f32)
            + from_sibling[place, rows].astype(f32)
        )
    for j in range(owners):
        block = grad_all.at[me, pl.ds(j * piece, piece)]
        pl.when(column != j)(
            lambda: copies.wait_recv(block, grad_piece_sems.at[j], sibling)
        )
    for other in all_rows:
        copies.send(grad_all.at[me], grad_all.at[me], grad_all_sems.at[me], {"row": other})
    for part, rows in enumerate(windows):
        value = total[rows]
        for k in range(groups - 1):
            copies.wait_recv(from_peer.at[k, rows], peer_sems.at[k, part], sibling)
            value = value + from_peer[k, rows].astype(f32)
        out_ref[rows] = value.astype(out_ref.dtype)
    for other in all_rows:
        copies.wait_recv(grad_all.at[other], grad_all_sems.at[other], sibling)
    shares = n_row // 2
    for j in range(n_row):
        ref = (grad_self_ref, grad_neigh_ref)[j // shares]
        ref[pl.ds(j % shares * chunk, chunk)] = grad_all[j].astype(f32)
    copies.finish()


def scatter_rows(partials, own_grad, share, n_row, n_col, scale):
    rows, width = own_grad.shape
    groups = n_row // 2
    others = max(groups - 1, 1)
    chunk = share.shape[0]
    piece = max(chunk // n_col, 16)
    owners = chunk // piece
    vmem = pl.BlockSpec(memory_space=pltpu.VMEM)
    bf16 = jnp.bfloat16
    dma = pltpu.SemaphoreType.DMA
    return pl.pallas_call(
        functools.partial(scatter_rows_kernel, n_row, n_col, scale),
        out_shape=(
            jax.ShapeDtypeStruct((rows, width), bf16),
            jax.ShapeDtypeStruct((width, width), jnp.float32),
            jax.ShapeDtypeStruct((width, width), jnp.float32),
        ),
        in_specs=[vmem] * 3,
        out_specs=(vmem,) * 3,
        scratch_shapes=[
            pltpu.VMEM((groups, rows, width), bf16),
            pltpu.VMEM((others, rows, width), bf16),
            pltpu.VMEM((others, rows, width), bf16),
            pltpu.VMEM((rows, width), jnp.float32),
            pltpu.VMEM((n_col - 1, piece, width), jnp.float32),
            pltpu.VMEM((n_row, chunk, width), bf16),
            dma((4 * groups + 2 * n_col + n_row,)),
            dma((groups, 2)),
            dma((others, 2)),
            dma((n_col - 1,)),
            dma((owners,)),
            dma((n_row,)),
        ],
        compiler_params=pltpu.CompilerParams(
            collective_id=2, has_side_effects=True, vmem_limit_bytes=VMEM_LIMIT
        ),
        name="scatter_rows",
    )(partials, own_grad, share)


def per_device(
    features, w_self, w_neigh, cotangent, degree, tile_rows, tile_cols, tile_edges, tile_count
):
    rows, width = features.shape
    tile = tile_edges.shape[2]
    slots = tile_rows.shape[0]
    n_row = lax.axis_size("row")
    n_col = lax.axis_size("col")
    edges = tile_edges
    padding = (-slots) % UNROLL
    if padding:
        edges = jnp.pad(edges, ((0, 0), (0, padding), (0, 0)))
        tile_rows = jnp.pad(tile_rows, (0, padding))
        tile_cols = jnp.pad(tile_cols, (0, padding))
    degree_wide = degree.astype(jnp.float32)[:, None]

    column_nodes = gather_rows(features, n_row)
    partial_sums = spread(
        True, tile_rows, tile_cols, tile_count, edges, column_nodes, rows * n_col // tile
    )
    activations, own_grad, share, row_nodes = layer_call(
        partial_sums.reshape(n_col, rows, width),
        features,
        w_self,
        w_neigh,
        cotangent,
        degree_wide,
        n_row,
        n_col,
    )
    partial_grads = spread(
        False, tile_rows, tile_cols, tile_count, edges, row_nodes, rows * n_row // tile
    )
    scale = 1.0 / math.sqrt(rows * n_row * n_col)
    feature_grad, grad_self, grad_neigh = scatter_rows(
        partial_grads.reshape(n_row, rows, width), own_grad, share, n_row, n_col, scale
    )
    return (activations, feature_grad, grad_self, grad_neigh)


def solution(mesh):
    nodes = P(("row", "col"), None)
    flat = P(("row", "col"))
    return jax.shard_map(
        per_device,
        mesh=mesh,
        in_specs=(nodes, P(), P(), nodes, flat, flat, flat, P(None, ("row", "col"), None), flat),
        out_specs=(nodes, nodes, P(), P()),
        check_vma=False,
    )
```
